32 devices in a mesh: dp: 4 (over z_hi, core), seq: 4 (over y, x), head: 2 (over z_lo).
Axes of the slice: x: 2, y: 2, z: 4 (z_hi: 2, z_lo: 2; z = z_hi * 2 + z_lo), core: 2. Of those that a mesh axis runs over, the one named last changes fastest.
Arguments:
- hidden_in: bfloat16 [8, 2048, 768], P('dp', ('seq', 'head')), may hold values from -6 to 6
- cotangent: bfloat16 [8, 2048, 768], P('dp', ('seq', 'head')), may hold values from -6 to 6
- lengths: int32 [8], P('dp'), may hold values from 512 to 2048, as said below
- w_qkv: float32 [768, 2304], P(None, 'dp'), may hold values from -0.21875 to 0.21875
- w_out: float32 [768, 768], P(None, 'dp'), may hold values from -1.25 to 1.25
- w_gated: float32 [768, 6144], P(None, 'dp'), may hold values from -0.21875 to 0.21875
- w_down: float32 [3072, 768], P('dp'), may hold values from -0.109375 to 0.109375
- vectors: float32 [11520], P('dp'), may hold values from -0.5 to 1.4, as said below
- mom_qkv: float32 [768, 2304], P(None, 'dp'), may hold values from -80 to 80
- mom_out: float32 [768, 768], P(None, 'dp'), may hold values from -80 to 80
- mom_gated: float32 [768, 6144], P(None, 'dp'), may hold values from -80 to 80
- mom_down: float32 [3072, 768], P('dp'), may hold values from -80 to 80
- vec_first: float32 [11520], P('dp'), may hold values from -40 to 40
- vec_second: float32 [11520], P('dp'), may hold values from 3.2768 to 13.1072
Outputs:
- hidden_out: bfloat16 [8, 2048, 768], P('dp', ('seq', 'head'))
- grad_in: bfloat16 [8, 2048, 768], P('dp', ('seq', 'head'))
- mom_qkv_new: float32 [768, 2304], P(None, 'dp')
- mom_out_new: float32 [768, 768], P(None, 'dp')
- mom_gated_new: float32 [768, 6144], P(None, 'dp')
- mom_down_new: float32 [3072, 768], P('dp')
- w_qkv_new: float32 [768, 2304], P(None, 'dp')
- w_out_new: float32 [768, 768], P(None, 'dp')
- w_gated_new: float32 [768, 6144], P(None, 'dp')
- w_down_new: float32 [3072, 768], P('dp')
- vec_first_new: float32 [11520], P('dp')
- vec_second_new: float32 [11520], P('dp')
- vectors_new: float32 [11520], P('dp')
The draws below stay inside these ranges and needn't reach their ends.
Inputs may be any that keep to these rules, and one draw needn't show every extreme that they name: `lengths`: in each aligned block of 2 entries, one entry, drawn from the seed, equals 2048. `vectors`: the two norm gains lie between 0.6 and 1.4, every bias between -0.5 and 0.5.
All inputs are finite; a program needn't handle non-finite values.
Results may differ from the reference program's by a relative error of at most 0.028.
Values may be sent and summed in bfloat16 or wider, within the bound.
No kernel may reach another device: no remote copies, remote signals or barrier semaphores. Data moves between devices by JAX's collectives and lax.ppermute only.
A program may use at most 320 MiB of HBM per device.

```python
import math
import jax
import jax.numpy as jnp
from jax import lax

D = 768
HEADS = 12
HEAD_DIM = 64
FF = 3072
SEQS = 2
NS_STEPS = 5
STEP = 10
LENGTH = 2048
BATCH = 8
TOKENS = 16384
VEC = 11520
N_DP = 4


def draw_lengths(key, part):
    key = jax.random.fold_in(key, 7)
    key_ragged, key_chosen = jax.random.split(key)
    groups = BATCH // SEQS
    ragged = jax.random.randint(key_ragged, (groups, SEQS), LENGTH // 4, LENGTH + 1)
    chosen = jax.random.randint(key_chosen, (groups,), 0, SEQS)
    slots = jnp.arange(SEQS)[None, :]
    filled = jnp.where(slots == chosen[:, None], LENGTH, ragged)
    return filled.reshape(BATCH).astype(jnp.int32)


def draw_vectors(key, part):
    key = jax.random.fold_in(key, 19)
    key_gains, key_biases = jax.random.split(key)
    gains = jax.random.uniform(key_gains, (VEC,), jnp.float32, 0.6, 1.4)
    biases = jax.random.uniform(key_biases, (VEC,), jnp.float32, -0.5, 0.5)
    index = jnp.arange(VEC)
    gain_one = (index >= 2 * D) & (index < 3 * D)
    gain_two = (index >= 5 * D + 2 * FF) & (index < 6 * D + 2 * FF)
    return jnp.where(gain_one | gain_two, gains, biases)


def block_scale(key, dims, shards, least, largest):
    factor_of, own = 1.0, jax.random.fold_in(key, 6)
    for position, parts in shards:
        steps = jnp.exp(jax.random.uniform(jax.random.fold_in(own, position), (parts,), jnp.float32, least / len(shards), largest / len(shards)))
        factor_of = factor_of * jnp.repeat(steps, dims[position] // parts).reshape([-1 if axis == position else 1 for axis in range(len(dims))])
    return factor_of


def gaussian(key, shape, scale, most, cuts=(), dtype=jnp.bfloat16):
    array = jax.random.normal(key, shape, jnp.float32) * scale
    if len(cuts) > 0:
        array = block_scale(key, shape, cuts, -0.22, 0.18) * array
    return jnp.clip(array, min=-most, max=most).astype(dtype)


def setup_inputs(seed: int = 0) -> dict:
    arg_keys = jax.random.split(jax.random.key(seed), 15)
    return {
        "hidden_in": gaussian(arg_keys[0], (BATCH, LENGTH, D), 1.0, 6.0, ((0, 4), (1, 8))),
        "cotangent": gaussian(arg_keys[1], (BATCH, LENGTH, D), 1.0, 6.0, ((0, 4), (1, 8))),
        "lengths": draw_lengths(jax.random.fold_in(arg_keys[14], 71), 0),
        "w_qkv": gaussian(arg_keys[3], (D, 3 * D), D ** -0.5, 0.21875, ((1, 4),), jnp.float32),
        "w_out": gaussian(arg_keys[4], (D, D), (D // 32) ** -0.5, 1.25, ((1, 4),), jnp.float32),
        "w_gated": gaussian(arg_keys[5], (D, 2 * FF), D ** -0.5, 0.21875, ((1, 4),), jnp.float32),
        "w_down": gaussian(arg_keys[6], (FF, D), FF ** -0.5, 0.109375, ((0, 4),), jnp.float32),
        "vectors": draw_vectors(jax.random.fold_in(arg_keys[14], 71), 0),
        "mom_qkv": gaussian(arg_keys[8], (D, 3 * D), (0.1 * TOKENS ** 0.5), 80.0, ((1, 4),), jnp.float32),
        "mom_out": gaussian(arg_keys[9], (D, D), (0.1 * TOKENS ** 0.5), 80.0, ((1, 4),), jnp.float32),
        "mom_gated": gaussian(arg_keys[10], (D, 2 * FF), (0.1 * TOKENS ** 0.5), 80.0, ((1, 4),), jnp.float32),
        "mom_down": gaussian(arg_keys[11], (FF, D), (0.1 * TOKENS ** 0.5), 80.0, ((0, 4),), jnp.float32),
        "vec_first": gaussian(arg_keys[12], (VEC,), (0.05 * TOKENS ** 0.5), 40.0, ((0, 4),), jnp.float32),
        "vec_second": jnp.clip(jnp.exp(math.log(13.1072) - 1.3862944 * jax.random.uniform(arg_keys[13], (VEC,), jnp.float32) ** block_scale(arg_keys[13], (VEC,), ((0, 4),), -0.2, 0.2)), 3.2768, 13.1072),
    }


HIGHEST = lax.Precision.HIGHEST
POLY_A = 3.4445
POLY_B = -4.775
POLY_C = 2.0315
MUON_BETA = 0.95
MUON_RATE = 0.3
MUON_DECAY = 0.01
ADAM_BETA_ONE = 0.9
ADAM_BETA_TWO = 0.999
ADAM_RATE = 0.4
ADAM_EPSILON = 1e-08
NORM_EPSILON = 1e-06
MASKED = -1e+30

@jax.custom_vjp
def low(v):
    return lax.optimization_barrier(v.astype(jnp.bfloat16)).astype(jnp.float32)

@jax.custom_vjp
def low_back(v):
    return v

def low_keep(v):
    return (low(v), None)

def low_pass(kept, grad):
    return (grad,)

def back_keep(v):
    return (v, None)

def back_low(kept, grad):
    return (low(grad),)
low.defvjp(low_keep, low_pass)
low_back.defvjp(back_keep, back_low)

def round_half(values):
    return lax.optimization_barrier(values.astype(jnp.bfloat16)).astype(jnp.float32)

def layer_norm(values, gain, shift):
    centre = values - lax.optimization_barrier(jnp.mean(values, -1, keepdims=True))
    spread = lax.optimization_barrier(jnp.mean(centre * centre, -1, keepdims=True))
    return centre * lax.rsqrt(spread + NORM_EPSILON) * gain + shift

def split_vectors(vector, width, hidden):
    base = 4 * width + 2 * hidden
    return (vector[:width], vector[width:2 * width], vector[2 * width:3 * width], vector[3 * width:4 * width], vector[4 * width:base], vector[base:base + width], vector[base + width:base + 2 * width], vector[base + 2 * width:base + 3 * width])

def head_slopes(first_head, count, heads, length):
    index = (first_head + jnp.arange(count)).astype(jnp.float32)
    return jnp.exp2(-8.0 * (index + 1.0) / heads) * (64.0 / length)

def attend_rows(query_rows, keys_all, values_all, row_start, valid_len, slopes):
    rows = query_rows.shape[0]
    count = keys_all.shape[0]
    inner = jnp.einsum('qhe,khe->hqk', query_rows, keys_all, precision=HIGHEST)
    inner = low_back(inner)
    query_pos = row_start + jnp.arange(rows)
    key_pos = jnp.arange(count)
    distance = jnp.abs(query_pos[:, None] - key_pos[None, :]).astype(jnp.float32)
    scores = inner * (1.0 / math.sqrt(query_rows.shape[-1])) - slopes[:, None, None] * distance[None]
    scores = jnp.where((key_pos < valid_len)[None, None, :], scores, MASKED)
    highest = lax.optimization_barrier(jnp.max(scores, -1, keepdims=True))
    weights = jnp.exp(scores - highest)
    weights = weights / lax.optimization_barrier(jnp.sum(weights, -1, keepdims=True))
    return jnp.einsum('hqk,khe->qhe', low(weights), values_all, precision=HIGHEST)

def sequence_forward(rows_in, valid_len, params, slopes):
    w_qkv, w_out, w_gated, w_down, vector = params
    width = rows_in.shape[1]
    hidden = w_down.shape[0]
    count = rows_in.shape[0]
    value_bias, out_bias, gain_one, shift_one, gated_bias, down_bias, gain_two, shift_two = split_vectors(vector, width, hidden)
    zero_bias = jnp.zeros((width,), jnp.float32)
    projected = jnp.dot(rows_in, w_qkv, precision=HIGHEST) + jnp.concatenate([zero_bias, zero_bias, value_bias])
    projected = low_back(low(projected))
    queries = projected[:, :width].reshape(count, HEADS, HEAD_DIM)
    keys_all = projected[:, width:2 * width].reshape(count, HEADS, HEAD_DIM)
    values_all = projected[:, 2 * width:].reshape(count, HEADS, HEAD_DIM)
    rows = min(512, count)
    starts = jnp.arange(count // rows) * rows
    query_blocks = queries.reshape(count // rows, rows, HEADS, HEAD_DIM)

    def one_block(item):
        return jax.checkpoint(attend_rows)(item[0], keys_all, values_all, item[1], valid_len, slopes)
    context = lax.map(one_block, (query_blocks, starts)).reshape(count, width)
    context = low_back(low(context))
    attended = low_back(jnp.dot(context, w_out, precision=HIGHEST) + out_bias)
    first = layer_norm(rows_in + attended, gain_one, shift_one)
    gated = low_back(jnp.dot(low(first), w_gated, precision=HIGHEST) + gated_bias)
    mixed = low(jax.nn.gelu(gated[:, :hidden], approximate=False) * gated[:, hidden:])
    ffn = low_back(jnp.dot(mixed, w_down, precision=HIGHEST) + down_bias)
    second = layer_norm(first + ffn, gain_two, shift_two)
    valid = (jnp.arange(count) < valid_len).astype(jnp.float32)
    return second * valid[:, None]

def gram_of(matrix, wide, blocks):
    if wide:
        pieces = matrix.reshape(matrix.shape[0], blocks, matrix.shape[1] // blocks)
        block_grams = jnp.einsum('ibk,jbk->bij', pieces, pieces, precision=HIGHEST)
    else:
        pieces = matrix.reshape(blocks, matrix.shape[0] // blocks, matrix.shape[1])
        block_grams = jnp.einsum('bki,bkj->bij', pieces, pieces, precision=HIGHEST)
    return lax.optimization_barrier(jnp.sum(round_half(block_grams), 0))

def orthogonalize(matrix, wide, blocks):
    gram = gram_of(matrix, wide, blocks)
    norm_value = jnp.sqrt(jnp.trace(gram)) + 1e-07
    current = matrix / norm_value
    gram = gram / (norm_value * norm_value)
    for turn in range(NS_STEPS):
        if turn > 0:
            gram = gram_of(current, wide, blocks)
        poly = POLY_B * gram + POLY_C * jnp.dot(gram, gram, precision=HIGHEST)
        if wide:
            current = POLY_A * current + jnp.dot(poly, current, precision=HIGHEST)
        else:
            current = POLY_A * current + jnp.dot(current, poly, precision=HIGHEST)
    return current

def muon_update(weight, momentum, gradient, wide):
    moment = MUON_BETA * momentum + gradient
    ortho = orthogonalize(moment, wide, N_DP)
    factor = 0.2 * math.sqrt(max(weight.shape[0], weight.shape[1]))
    return (moment, weight * (1.0 - MUON_RATE * MUON_DECAY) - MUON_RATE * factor * ortho)

def reference(hidden_in, cotangent, lengths, w_qkv, w_out, w_gated, w_down, vectors, mom_qkv, mom_out, mom_gated, mom_down, vec_first, vec_second):
    slopes = head_slopes(0, HEADS, HEADS, LENGTH)
    masters = (w_qkv, w_out, w_gated, w_down, vectors)

    def forward(inputs, params):
        lowered = tuple((low(item) for item in params))
        return lax.map(lambda item: sequence_forward(item[0], item[1], lowered, slopes), (inputs, lengths))
    outputs, pull = jax.vjp(forward, hidden_in.astype(jnp.float32), masters)
    grad_x, grads = pull(cotangent.astype(jnp.float32))
    mom_qkv_new, w_qkv_new = muon_update(w_qkv, mom_qkv, grads[0], True)
    mom_out_new, w_out_new = muon_update(w_out, mom_out, grads[1], True)
    mom_gated_new, w_gated_new = muon_update(w_gated, mom_gated, grads[2], True)
    mom_down_new, w_down_new = muon_update(w_down, mom_down, grads[3], False)
    grad_vec = grads[4]
    first_new = ADAM_BETA_ONE * vec_first + (1.0 - ADAM_BETA_ONE) * grad_vec
    second_new = ADAM_BETA_TWO * vec_second + (1.0 - ADAM_BETA_TWO) * grad_vec * grad_vec
    first_hat = first_new / (1.0 - ADAM_BETA_ONE ** STEP)
    second_hat = second_new / (1.0 - ADAM_BETA_TWO ** STEP)
    vectors_new = vectors - ADAM_RATE * first_hat / (jnp.sqrt(second_hat) + ADAM_EPSILON)
    return (outputs.astype(jnp.bfloat16), grad_x.astype(jnp.bfloat16), mom_qkv_new, mom_out_new, mom_gated_new, mom_down_new, w_qkv_new, w_out_new, w_gated_new, w_down_new, first_new, second_new, vectors_new)
```

```python
import functools
import math

import jax
import jax.numpy as jnp
from jax import lax
from jax.experimental import pallas as pl
from jax.experimental.pallas import tpu as pltpu
from jax.sharding import PartitionSpec as P

D = 768
HEADS = 12
HEAD_DIM = 64
FF = 3072
NS_STEPS = 5
STEP = 10

POLY_A = 3.4445
POLY_B = -4.775
POLY_C = 2.0315
MUON_BETA = 0.95
MUON_RATE = 0.3
MUON_DECAY = 0.01
ADAM_BETA_ONE = 0.9
ADAM_BETA_TWO = 0.999
ADAM_RATE = 0.4
ADAM_EPSILON = 1e-08
NORM_EPSILON = 1e-06
MASKED = -1e30

BF = jnp.bfloat16
F32 = jnp.float32
AXES = ("dp", "seq", "head")
VMEM_LIMIT = 60 * 1024 * 1024
NT = (((1,), (1,)), ((), ()))
NN = (((1,), (0,)), ((), ()))
TN = (((0,), (0,)), ((), ()))


def dot(a, b, dims=NN):
    return lax.dot_general(a, b, dims, preferred_element_type=F32)


def split_three(value):
    high = value.astype(BF)
    rest = value - high.astype(F32)
    mid = rest.astype(BF)
    low = (rest - mid.astype(F32)).astype(BF)
    return high.astype(F32), mid.astype(F32), low.astype(F32)


def after(value, *others):
    hbm = pl.BlockSpec(memory_space=pl.ANY)
    return pl.pallas_call(
        lambda *refs: None,
        out_shape=jax.ShapeDtypeStruct(value.shape, value.dtype),
        in_specs=[hbm] * (1 + len(others)),
        out_specs=hbm,
        input_output_aliases={0: 0},
        name="after",
    )(value, *others)


def unfold(ref, block, at, count):
    columns = ref.shape[2] // 2
    return jnp.concatenate([ref[block, :, at : at + count], ref[block, :, columns + at : columns + at + count]], 0)


def fold(ref, block, at, value):
    columns = ref.shape[2] // 2
    half = value.shape[0] // 2
    count = value.shape[1]
    ref[block, :, at : at + count] = value[:half].astype(ref.dtype)
    ref[block, :, columns + at : columns + at + count] = value[half:].astype(ref.dtype)


def sum_split_kernel(places, pairs, with_vector, bits_ref, *refs):
    ins = refs[: 2 * pairs]
    vector = refs[2 * pairs : 2 * pairs + 2]
    outs = refs[len(refs) - 2 * len(places) - with_vector :]
    for place, (pair, low, high, axis, which) in enumerate(places):
        mine = 0 if which is None else bits_ref[which]
        for other, out in enumerate(outs[2 * place : 2 * place + 2]):
            at = mine if other == 0 else 1 - mine
            index = (slice(None),) * axis + (at, Ellipsis, slice(low, high))
            first, second = ins[2 * pair], ins[2 * pair + 1]
            out[...] = (first[index].astype(F32) + second[index].astype(F32)).astype(BF)
    if with_vector:
        outs[-1][...] = vector[0][...] + vector[1][...]


def sum_split(places, bits, pairs, vector=None, waits=()):
    smem = pl.BlockSpec(memory_space=pltpu.SMEM)
    by_half = min(place[3] for place in places) > 0
    arrays = [array for pair in pairs for array in pair]
    shapes = []
    for pair, low, high, axis, which in places:
        shape = pairs[pair][0].shape
        shape = shape[:axis] + shape[axis + 1 : -1] + (high - low,)
        shapes += [jax.ShapeDtypeStruct(shape, BF)] * 2

    def spec(array):
        if by_half:
            return pl.BlockSpec((1,) + array.shape[1:], lambda z: (z,) + (0,) * (len(array.shape) - 1))
        return pl.BlockSpec(memory_space=pltpu.VMEM)

    def whole(array):
        if by_half:
            return pl.BlockSpec(array.shape, lambda z: (0,) * len(array.shape))
        return pl.BlockSpec(memory_space=pltpu.VMEM)

    in_specs = [smem] + [spec(array) for array in arrays]
    out_specs = [spec(shape) for shape in shapes]
    if vector:
        arrays += list(vector)
        in_specs += [whole(vector[0])] * 2
        shapes.append(jax.ShapeDtypeStruct(vector[0].shape, F32))
        out_specs.append(whole(vector[0]))
    return pl.pallas_call(
        functools.partial(sum_split_kernel, places, len(pairs), 1 if vector else 0),
        grid=(2,) if by_half else (),
        out_shape=tuple(shapes),
        in_specs=in_specs + [pl.BlockSpec(memory_space=pl.ANY)] * len(waits),
        out_specs=tuple(out_specs),
        compiler_params=pltpu.CompilerParams(vmem_limit_bytes=VMEM_LIMIT),
        cost_estimate=pl.CostEstimate(
            flops=0, bytes_accessed=sum(3 * 2 * p[0].size for p in pairs), transcendentals=0
        ),
        name="sum_split",
    )(bits, *arrays, *waits)


def join_kernel(places, bits_ref, *refs):
    count = len(places)
    outs = refs[-count:]
    for index, (axis, which) in enumerate(places):
        before = (slice(None),) * axis
        mine = bits_ref[which]
        outs[index][before + (mine,)] = refs[index][before + (0,)]
        outs[index][before + (1 - mine,)] = refs[count + index][before + (0,)]


def join_pairs(places, bits, mine, others, waits=()):
    vmem = pl.BlockSpec(memory_space=pltpu.VMEM)
    smem = pl.BlockSpec(memory_space=pltpu.SMEM)
    shapes = tuple(
        jax.ShapeDtypeStruct(array.shape[:axis] + (2,) + array.shape[axis + 1 :], array.dtype)
        for array, (axis, which) in zip(mine, places)
    )
    return pl.pallas_call(
        functools.partial(join_kernel, places),
        out_shape=shapes,
        in_specs=[smem] + [vmem] * (2 * len(mine)) + [pl.BlockSpec(memory_space=pl.ANY)] * len(waits),
        out_specs=(vmem,) * len(mine),
        compiler_params=pltpu.CompilerParams(vmem_limit_bytes=VMEM_LIMIT),
        cost_estimate=pl.CostEstimate(
            flops=0, bytes_accessed=sum(8 * array.size for array in mine), transcendentals=0
        ),
        name="join_pairs",
    )(bits, *mine, *others, *waits)


def key_features(keys, start, rows, length):
    lane = lax.broadcasted_iota(jnp.int32, (rows, 128), 1)
    pos = start + lax.broadcasted_iota(jnp.int32, (rows, 128), 0)
    low = jnp.bitwise_and(pos, 255)
    feats = jnp.where(lane < 68, (pos - low).astype(F32), jnp.where(lane < 71, low.astype(F32), 1.0))
    feats = jnp.where(lane == 64, jnp.where(pos >= length, MASKED, 0.0), feats)
    wide = jnp.concatenate([keys.astype(F32), jnp.zeros_like(keys, F32)], 1)
    return jnp.where(lane < 64, wide, jnp.where(lane < 77, feats, 0.0))


def query_features(queries, start, rows, slope, log_total):
    lane = lax.broadcasted_iota(jnp.int32, (rows, 128), 1)
    first = lax.broadcasted_iota(jnp.int32, (1, 128), 1)
    pos = (start + lax.broadcasted_iota(jnp.int32, (rows, 128), 0)).astype(F32)
    tilt = jnp.zeros((1, 128), F32)
    for offset, piece in enumerate(split_three(jnp.full((1, 128), slope, F32))):
        tilt = jnp.where((first == 65 + offset) | (first == 68 + offset), -piece, tilt)
    tilt = jnp.broadcast_to(tilt, (rows, 128))
    for offset, piece in enumerate(split_three(pos * slope)):
        tilt = jnp.where(lane == 71 + offset, piece, tilt)
    base = jnp.concatenate([queries.astype(F32) * (1.0 / math.sqrt(HEAD_DIM)), jnp.zeros_like(queries, F32)], 1)
    base = jnp.where(lane == 64, 1.0, base)
    if log_total is not None:
        for offset, piece in enumerate(split_three(log_total)):
            base = jnp.where(lane == 74 + offset, -piece, base)
    return base, tilt


def distances(slope, rows):
    row = lax.broadcasted_iota(jnp.int32, (2 * rows, rows), 0)
    col = lax.broadcasted_iota(jnp.int32, (2 * rows, rows), 1)
    first = jnp.abs(row - col).astype(F32) * slope
    second = jnp.abs(row - col - rows).astype(F32) * slope
    return jnp.zeros_like(first), first, second


def relation(pair, block, mine):
    start = jnp.bitwise_xor(2 * pair, mine)
    other = jnp.bitwise_xor(block, mine)
    behind = jnp.where(start > other, 1, 0)
    before = jnp.where(start + 1 < other, 1, 0)
    return jnp.where(behind + before == 0, 1 + other - start, 0), behind - before


def with_ones(values, count):
    rows = values.shape[0]
    lane = lax.broadcasted_iota(jnp.int32, (rows, 128), 1)
    wide = jnp.concatenate([values.astype(F32), jnp.zeros_like(values, F32)], 1)
    return jnp.where(lane < 64, wide, jnp.where(lane < 64 + count, 1.0, 0.0)).astype(BF)


def attention_forward_kernel(
    rows, q_blocks, k_blocks, heads, info_ref, slope_ref, qkv_ref, out_ref, low_ref, log_ref, q_s, k_s, v_s, t_s, o_s
):
    mine = info_ref[0]
    length = info_ref[1]
    narrow = heads * HEAD_DIM
    for h in range(heads):
        lo = h * HEAD_DIM

        @pl.loop(0, k_blocks)
        def _(r):
            rs = pl.ds(pl.multiple_of(r * rows, rows), rows)
            start = jnp.bitwise_xor(r, mine) * rows
            keys = key_features(unfold(qkv_ref, r, narrow + lo, HEAD_DIM), start, rows, length)
            k_s[h, r] = keys.T.astype(BF)
            v_s[h, rs] = with_ones(unfold(qkv_ref, r, 2 * narrow + lo, HEAD_DIM), 1)

        @pl.loop(0, q_blocks)
        def _(r):
            rs = pl.ds(pl.multiple_of(r * rows, rows), rows)
            start = jnp.bitwise_xor(r, mine) * rows
            queries = unfold(qkv_ref, r, lo, HEAD_DIM)
            base, tilt = query_features(queries, start, rows, slope_ref[h], None)
            q_s[h, 0, rs] = (base - tilt).astype(BF)
            q_s[h, 1, rs] = base.astype(BF)
            q_s[h, 2, rs] = (base + tilt).astype(BF)

        for index, value in enumerate(distances(slope_ref[h], rows)):
            t_s[h, index] = value

    wide = 2 * rows

    def attend(h, pair):
        rs = pl.ds(pl.multiple_of(pair * wide, wide), wide)
        scores = []
        for kb in range(k_blocks):
            index, side = relation(pair, kb, mine)
            scores.append(dot(q_s[h, 1 - side, rs], k_s[h, kb]) - t_s[h, index])
        high = scores[0]
        for s in scores[1:]:
            high = jnp.maximum(high, s)
        high = jnp.max(high, -1, keepdims=True)
        weights = jnp.concatenate([jnp.exp(s - high).astype(BF) for s in scores], 1)
        total = dot(weights, v_s[h])
        norm = total[:, HEAD_DIM : HEAD_DIM + 1]
        return total[:, :HEAD_DIM] / norm, high + jnp.log(norm)

    lane = lax.broadcasted_iota(jnp.int32, (wide, 128), 1)
    if q_blocks == k_blocks:

        @pl.loop(0, q_blocks // 2)
        def _(pair):
            rs = pl.ds(pl.multiple_of(pair * wide, wide), wide)
            results = [attend(h, pair) for h in range(heads)]
            logs = jnp.zeros((wide, 128), F32)
            for h, (value, log) in enumerate(results):
                o_s[h, rs] = value
                logs = jnp.where(lane == h, log, logs)
            log_ref[rs] = logs

    else:
        log_ref[...] = jnp.zeros_like(log_ref)

        @pl.loop(0, heads * q_blocks // 2)
        def _(step):
            h = step // (q_blocks // 2)
            pair = lax.rem(step, q_blocks // 2)
            rs = pl.ds(pl.multiple_of(pair * wide, wide), wide)
            value, log = attend(h, pair)
            o_s[h, rs] = value
            log_ref[rs] = jnp.where(lane == h, log, log_ref[rs])

    for h in range(heads):
        out_ref[:, h * HEAD_DIM : (h + 1) * HEAD_DIM] = o_s[h]
        for r in range(q_blocks):
            fold(low_ref, r, h * HEAD_DIM, o_s[h, r * rows : (r + 1) * rows])


def attention_forward(info, slopes, qkv, rows, q_blocks):
    heads = qkv.shape[2] // (6 * HEAD_DIM)
    k_blocks = qkv.shape[0]
    q_rows = q_blocks * rows
    vmem = pl.BlockSpec(memory_space=pltpu.VMEM)
    smem = pl.BlockSpec(memory_space=pltpu.SMEM)
    return pl.pallas_call(
        functools.partial(attention_forward_kernel, rows, q_blocks, k_blocks, heads),
        out_shape=(
            jax.ShapeDtypeStruct((q_rows, heads * HEAD_DIM), F32),
            jax.ShapeDtypeStruct((q_blocks, rows // 2, 2 * heads * HEAD_DIM), BF),
            jax.ShapeDtypeStruct((q_rows, 128), F32),
        ),
        in_specs=[smem, smem, vmem],
        out_specs=(vmem, vmem, vmem),
        scratch_shapes=[
            pltpu.VMEM((heads, 3, q_rows, 128), BF),
            pltpu.VMEM((heads, k_blocks, 128, rows), BF),
            pltpu.VMEM((heads, k_blocks * rows, 128), BF),
            pltpu.VMEM((heads, 3, 2 * rows, rows), F32),
            pltpu.VMEM((heads, q_rows, HEAD_DIM), F32),
        ],
        compiler_params=pltpu.CompilerParams(vmem_limit_bytes=VMEM_LIMIT),
        cost_estimate=pl.CostEstimate(
            flops=16 * heads * q_rows * k_blocks * rows * HEAD_DIM, bytes_accessed=6_000_000, transcendentals=0
        ),
        name="attention_forward",
    )(info, slopes, qkv)


def attention_backward_kernel(
    rows,
    q_blocks,
    k_blocks,
    heads,
    head,
    info_ref,
    slope_ref,
    qkv_ref,
    att_ref,
    log_ref,
    grad_ref,
    *rest,
):
    out_ref, q_s, qt_s, k_s, v_s, g_s, gt_s, t_s, kt_s, dq_s, dk_s, dv_s = rest[-12:]
    mine = info_ref[0]
    length = info_ref[1]
    narrow = heads * HEAD_DIM
    scale = 1.0 / math.sqrt(HEAD_DIM)
    lo = head * HEAD_DIM
    slope = slope_ref[head]

    @pl.loop(0, k_blocks)
    def _(r):
        rs = pl.ds(pl.multiple_of(r * rows, rows), rows)
        start = jnp.bitwise_xor(r, mine) * rows
        keys = unfold(qkv_ref, r, narrow + lo, HEAD_DIM)
        k_s[rs] = key_features(keys, start, rows, length).astype(BF)
        kt_s[r // 2, lax.rem(r, 2)] = keys.astype(F32).T.astype(BF)
        v_s[rs] = with_ones(unfold(qkv_ref, r, 2 * narrow + lo, HEAD_DIM), 3)

    @pl.loop(0, q_blocks)
    def _(r):
        rs = pl.ds(pl.multiple_of(r * rows, rows), rows)
        start = jnp.bitwise_xor(r, mine) * rows
        queries = unfold(qkv_ref, r, lo, HEAD_DIM)
        log_total = log_ref[rs, head : head + 1]
        base, tilt = query_features(queries, start, rows, slope, log_total)
        q_s[rs] = base.astype(BF)
        base = base.T
        tilt = tilt.T
        qt_s[0, r] = (base - tilt).astype(BF)
        qt_s[1, r] = base.astype(BF)
        qt_s[2, r] = (base + tilt).astype(BF)
        grads = unfold(grad_ref, r, lo, HEAD_DIM).astype(F32)
        delta = jnp.sum(grads * att_ref[rs, lo : lo + HEAD_DIM], -1, keepdims=True)
        lane = lax.broadcasted_iota(jnp.int32, (rows, 128), 1)
        wide = jnp.concatenate([grads, jnp.zeros_like(grads)], 1)
        for offset, piece in zip((64, 65, 66), split_three(delta)):
            wide = jnp.where(lane == offset, -piece, wide)
        g_s[rs] = wide.astype(BF)
        gt_s[r] = wide.T.astype(BF)

    for index, value in enumerate(distances(slope, rows)):
        t_s[index] = value
    dq_s[...] = jnp.zeros_like(dq_s)
    wide = 2 * rows

    @pl.loop(0, k_blocks // 2)
    def _(pair):
        ks = pl.ds(pl.multiple_of(pair * wide, wide), wide)
        keys = k_s[ks]
        values = v_s[ks]
        weights, grad_scores = [], []
        for qb in range(q_blocks):
            index, side = relation(pair, qb, mine)
            w = jnp.exp(dot(keys, qt_s[1 + side, qb]) - t_s[index])
            grad_scores.append((w * dot(values, gt_s[qb])).astype(BF))
            weights.append(w.astype(BF))
        grad_scores = jnp.concatenate(grad_scores, 1)
        dv_s[ks] = dot(jnp.concatenate(weights, 1), g_s[...])[:, :HEAD_DIM]
        dk_s[ks] = dot(grad_scores, q_s[...])[:, :HEAD_DIM]
        dq_s[...] += dot(jnp.concatenate([kt_s[pair, 0], kt_s[pair, 1]], 1), grad_scores)

    for r in range(k_blocks):
        rs = slice(r * rows, (r + 1) * rows)
        if r < q_blocks:
            fold(out_ref, r, 0, dq_s[:, rs].T * scale)
        else:
            fold(out_ref, r, 0, jnp.zeros((rows, HEAD_DIM), F32))
        fold(out_ref, r, HEAD_DIM, dk_s[rs])
        fold(out_ref, r, 2 * HEAD_DIM, dv_s[rs])


def attention_backward(head, info, slopes, qkv, attention, log_total, grads, rows, q_blocks, *others):
    heads = qkv.shape[2] // (6 * HEAD_DIM)
    k_blocks = qkv.shape[0]
    q_rows = q_blocks * rows
    k_rows = k_blocks * rows
    vmem = pl.BlockSpec(memory_space=pltpu.VMEM)
    smem = pl.BlockSpec(memory_space=pltpu.SMEM)
    hbm = pl.BlockSpec(memory_space=pl.ANY)
    return pl.pallas_call(
        functools.partial(attention_backward_kernel, rows, q_blocks, k_blocks, heads, head),
        out_shape=jax.ShapeDtypeStruct((k_blocks, rows // 2, 6 * HEAD_DIM), BF if k_blocks == q_blocks else F32),
        in_specs=[smem, smem, vmem, vmem, vmem, vmem] + [hbm] * len(others),
        out_specs=vmem,
        scratch_shapes=[
            pltpu.VMEM((q_rows, 128), BF),
            pltpu.VMEM((3, q_blocks, 128, rows), BF),
            pltpu.VMEM((k_rows, 128), BF),
            pltpu.VMEM((k_rows, 128), BF),
            pltpu.VMEM((q_rows, 128), BF),
            pltpu.VMEM((q_blocks, 128, rows), BF),
            pltpu.VMEM((3, 2 * rows, rows), F32),
            pltpu.VMEM((k_blocks // 2, 2, HEAD_DIM, rows), BF),
            pltpu.VMEM((HEAD_DIM, q_rows), F32),
            pltpu.VMEM((k_rows, HEAD_DIM), F32),
            pltpu.VMEM((k_rows, HEAD_DIM), F32),
        ],
        compiler_params=pltpu.CompilerParams(vmem_limit_bytes=VMEM_LIMIT),
        cost_estimate=pl.CostEstimate(
            flops=80 * q_rows * k_rows * HEAD_DIM, bytes_accessed=7_000_000, transcendentals=0
        ),
        name="attention_backward",
    )(info, slopes, qkv, attention, log_total, grads, *others)


def split_into(high_ref, low_ref, value):
    high = value.astype(BF)
    high_ref[...] = high
    if low_ref is not None:
        low_ref[...] = (value - high.astype(F32)).astype(BF)


PAIRS = ((0, 0), (1, 1), (2, 2), (0, 1), (0, 2), (1, 2))


def newton_schulz_steps(gram_ref, a0h, a0l, ah, al, bh, bl, qh, ql, q_s, a_s, p_s):
    size = gram_ref.shape[0]
    tile = 256
    count = size // tile
    row = lax.broadcasted_iota(jnp.int32, (size, size), 0)
    col = lax.broadcasted_iota(jnp.int32, (size, size), 1)
    eye = (row == col).astype(F32)
    trace = jnp.sum(jnp.sum(gram_ref[...] * eye, 0, keepdims=True), 1, keepdims=True)
    norm = jnp.sqrt(trace) + 1e-07
    a_s[...] = gram_ref[...] / (norm * norm)
    split_into(a0h, a0l, a_s[...])
    split_into(ah, al, a_s[...])

    def product(target, xh, xl, yh, yl, full, mirror, turned=False):
        for i in range(count):
            ri = slice(i * tile, (i + 1) * tile)
            for k in range(i if mirror else 0, count):
                rk = slice(k * tile, (k + 1) * tile)

                def term(x, y):
                    return dot(x[ri], y[rk], NT) if turned else dot(x[ri], y[:, rk])

                part = term(xh, yh)
                if full:
                    part = part + (term(xh, yl) + term(xl, yh))
                target[ri, rk] = part
                if mirror and k > i:
                    target[rk, ri] = part.T

    def advance(full, gram_full, first=False, last=False):
        product(p_s, ah, al, ah, al, full, True)
        poly = POLY_B * a_s[...] + POLY_C * p_s[...]
        if first:
            q_s[...] = poly + POLY_A * eye
        else:
            split_into(bh, bl if full else None, poly)
            product(p_s, bh, bl, qh, ql, full, False)
            q_s[...] = POLY_A * q_s[...] + p_s[...]
        if not last:
            split_into(qh, ql, q_s[...])
            product(p_s, a0h, a0l, qh, ql, gram_full, False, True)
            split_into(bh, bl, p_s[...])
            product(a_s, qh, ql, bh, bl, gram_full, True)
            split_into(ah, al, a_s[...])

    advance(False, False, first=True)

    @pl.loop(1, NS_STEPS - 2)
    def _(turn):
        advance(False, True)

    advance(True, True)
    advance(True, True, last=True)
    return norm


def ns_scratch(size):
    return [pltpu.VMEM((size, size), BF)] * 8 + [pltpu.VMEM((size, size), F32)] * 3


def newton_schulz_kernel(whole, which_ref, packed_ref, mine_ref, theirs_ref, *rest):
    out_ref, gram_s = rest[-13:-11]
    scratch = rest[-11:]
    tile = packed_ref.shape[3]
    half = tile // 2

    @pl.when(which_ref[0] == whole)
    def _():
        gram_s[...] = dot(mine_ref[...], mine_ref[...], NT) + dot(theirs_ref[...], theirs_ref[...], NT)

    @pl.when(which_ref[0] != whole)
    def _():
        for index, (i, k) in enumerate(PAIRS):
            block = jnp.concatenate([packed_ref[0, index], packed_ref[1, index]], 0)
            gram_s[i * tile : (i + 1) * tile, k * tile : (k + 1) * tile] = block
            if i != k:
                gram_s[k * tile : (k + 1) * tile, i * tile : (i + 1) * tile] = block.T

    norm = newton_schulz_steps(gram_s, *scratch)
    out_ref[...] = (scratch[8][...] / norm).astype(out_ref.dtype)


def newton_schulz(which, packed, mine, theirs, whole, *others):
    size = mine.shape[0]
    vmem = pl.BlockSpec(memory_space=pltpu.VMEM)
    smem = pl.BlockSpec(memory_space=pltpu.SMEM)
    return pl.pallas_call(
        functools.partial(newton_schulz_kernel, whole),
        out_shape=jax.ShapeDtypeStruct((size, size), BF),
        in_specs=[smem] + [vmem] * 3 + [pl.BlockSpec(memory_space=pl.ANY)] * len(others),
        out_specs=vmem,
        scratch_shapes=[pltpu.VMEM((size, size), F32)]
        + [pltpu.VMEM((size, size), BF)] * 8
        + [pltpu.VMEM((size, size), F32)] * 3,
        compiler_params=pltpu.CompilerParams(vmem_limit_bytes=VMEM_LIMIT),
        cost_estimate=pl.CostEstimate(flops=80 * size**3, bytes_accessed=7_000_000, transcendentals=0),
        name="newton_schulz",
    )(which, packed, mine, theirs, *others)


def gram_kernel(gated, out, which_ref, first_ref, second_ref, down_ref, packed_ref):
    tile = packed_ref.shape[3]
    half = tile // 2
    rest = gated - first_ref.shape[1]
    kinds = (
        lambda ri, rk: dot(first_ref[ri], first_ref[rk], NT) + dot(second_ref[ri, :rest], second_ref[rk, :rest], NT),
        lambda ri, rk: dot(down_ref[:, ri], down_ref[:, rk], TN),
        lambda ri, rk: dot(second_ref[ri, rest : rest + out], second_ref[rk, rest : rest + out], NT),
    )
    for index, gram in enumerate(kinds):

        @pl.when(jnp.minimum(which_ref[0], 2) == index)
        def _():
            for place, (i, k) in enumerate(PAIRS):
                block = gram(slice(i * tile, (i + 1) * tile), slice(k * tile, (k + 1) * tile))
                packed_ref[0, place] = block[:half]
                packed_ref[1, place] = block[half:]


def upper_gram(which, first, second, down, gated, out):
    vmem = pl.BlockSpec(memory_space=pltpu.VMEM)
    smem = pl.BlockSpec(memory_space=pltpu.SMEM)
    return pl.pallas_call(
        functools.partial(gram_kernel, gated, out),
        out_shape=jax.ShapeDtypeStruct((2, 6, 128, 256), F32),
        in_specs=[smem] + [vmem] * 3,
        out_specs=vmem,
        compiler_params=pltpu.CompilerParams(vmem_limit_bytes=VMEM_LIMIT),
        cost_estimate=pl.CostEstimate(flops=2 * first.shape[0] ** 2 * gated, bytes_accessed=6_000_000, transcendentals=0),
        name="upper_gram",
    )(which, first, second, down)


def update_kernel(scales, place_ref, *refs):
    halves, others = refs[:4], refs[4:8]
    first_ref, second_ref, down_ref, qkv_ref = refs[8:12]
    w_gated, w_down, w_out, w_qkv = refs[12:16]
    n_gated, n_down, n_out, n_qkv = refs[16:20]
    f_s, sems = refs[20:]
    which = place_ref[0]
    core = place_ref[1]
    half = halves[0].shape[0]
    copies = []
    for index, (mine, theirs) in enumerate(zip(halves, others)):
        m = jnp.bitwise_xor(which, index)
        for k, (ref, at) in enumerate(((mine, core), (theirs, 1 - core))):
            copy = pltpu.make_async_copy(
                ref, f_s.at[m, pl.ds(pl.multiple_of(at * half, half), half)], sems.at[2 * index + k]
            )
            copy.start()
            copies.append(copy)
    for copy in copies:
        copy.wait()
    third = first_ref.shape[1]
    gated = w_gated.shape[1] - third
    out = gated + w_out.shape[0]
    turned = (((0,), (1,)), ((), ()))

    def new(weight, scale, ortho):
        return weight * (1.0 - MUON_RATE * MUON_DECAY) - scale * ortho

    n_gated[:, :third] = new(w_gated[:, :third], scales[0], dot(f_s[0], first_ref[...]))
    n_gated[:, third:] = new(w_gated[:, third:], scales[0], dot(f_s[0], second_ref[:, :gated]))
    n_down[...] = new(w_down[...], scales[1], dot(down_ref[...], f_s[1], NT))
    n_out[...] = new(w_out[...], scales[2], dot(second_ref[:, gated:out], f_s[2], turned))
    n_qkv[...] = new(w_qkv[...], scales[3], dot(qkv_ref[...], f_s[3], turned))


def update(scales, place, halves, others, momenta, weights):
    size = halves[0].shape[1]
    vmem = pl.BlockSpec(memory_space=pltpu.VMEM)
    smem = pl.BlockSpec(memory_space=pltpu.SMEM)
    hbm = pl.BlockSpec(memory_space=pl.ANY)
    return pl.pallas_call(
        functools.partial(update_kernel, scales),
        out_shape=tuple(jax.ShapeDtypeStruct(weight.shape, F32) for weight in weights),
        in_specs=[smem] + [hbm] * 8 + [vmem] * 8,
        out_specs=(vmem,) * 4,
        scratch_shapes=[pltpu.VMEM((4, size, size), BF), pltpu.SemaphoreType.DMA((8,))],
        compiler_params=pltpu.CompilerParams(vmem_limit_bytes=VMEM_LIMIT),
        cost_estimate=pl.CostEstimate(flops=8 * size**3, bytes_accessed=28_000_000, transcendentals=0),
        name="update",
    )(place, *halves, *others, *momenta, *weights)


def project_kernel(
    groups, info_ref, vec_ref, x_ref, own_ref, far_ref, own_two, far_two, out_ref, group_ref, wo_ref, w_s, o_s
):
    core = info_ref[0]
    far = info_ref[1]
    unit = w_s.shape[2]
    seqs = out_ref.shape[0] // groups
    tokens = x_ref.shape[0] // seqs
    for a, refs in enumerate(((own_ref, far_ref), (own_two, far_two))):
        for z, ref in enumerate(refs):
            c = 2 * jnp.bitwise_xor(far, z) + jnp.bitwise_xor(core, a)
            for i in range(3):
                w_s[3 * c + i] = ref[:, i * unit : (i + 1) * unit]
            o_s[c] = ref[:, 3 * unit :]
    for g in range(groups):
        for role in range(3):
            group_ref[g, :, role * unit : (role + 1) * unit] = w_s[role * groups + g]
        part = dot(x_ref[...], group_ref[g])
        bias = jnp.concatenate(
            [jnp.zeros((1, 2 * unit), F32), vec_ref[0:1, g * unit : (g + 1) * unit]], 1
        )
        part = (part + bias).astype(BF)
        for b in range(seqs):
            fold(out_ref, b * groups + g, 0, part[b * tokens : (b + 1) * tokens])
    for c in range(4):
        wo_ref[:, c * unit : (c + 1) * unit] = o_s[c]


def project(info, vec, x, weights, groups, tokens):
    rows, width = x.shape
    unit = width // 4
    vmem = pl.BlockSpec(memory_space=pltpu.VMEM)
    smem = pl.BlockSpec(memory_space=pltpu.SMEM)
    return pl.pallas_call(
        functools.partial(project_kernel, groups),
        out_shape=(
            jax.ShapeDtypeStruct((groups * rows // tokens, tokens // 2, 6 * unit), BF),
            jax.ShapeDtypeStruct((groups, width, 3 * unit), BF),
            jax.ShapeDtypeStruct((width, width), BF),
        ),
        in_specs=[smem] + [vmem] * 6,
        out_specs=(vmem,) * 3,
        scratch_shapes=[pltpu.VMEM((12, width, unit), BF), pltpu.VMEM((4, width, unit), BF)],
        compiler_params=pltpu.CompilerParams(vmem_limit_bytes=VMEM_LIMIT),
        cost_estimate=pl.CostEstimate(
            flops=6 * rows * width * width, bytes_accessed=16_000_000, transcendentals=0
        ),
        name="project",
    )(info, vec, x, *weights)


def norm_back(grad, hat, scale, gain):
    inner = grad * gain
    mean = jnp.mean(inner, -1, keepdims=True)
    along = jnp.mean(inner * hat, -1, keepdims=True)
    return scale * (inner - mean - hat * along)


def feed_forward_kernel(
    groups,
    info_ref,
    vec_ref,
    x_ref,
    ctx_ref,
    cot_ref,
    wo_ref,
    own_ref,
    far_ref,
    own_two,
    far_two,
    out_ref,
    one_ref,
    gctx_ref,
    gvec_ref,
    keep_a,
    send_a,
    keep_b,
    send_b,
    w_s,
    ctx_s,
    hat_one,
    first_s,
    acc_s,
    gate_s,
    up_s,
    stage,
    wo_s,
    ffn_s,
    mixed_s,
    ggate_s,
    gup_s,
    sems,
):
    core = info_ref[0]
    far = info_ref[1]
    start = info_ref[2]
    rows, width = x_ref.shape
    unit = width // groups
    tokens = 2 * ctx_ref.shape[1]
    seqs = rows // tokens
    loads = []
    for a, refs in enumerate(((own_ref, far_ref), (own_two, far_two))):
        for z, ref in enumerate(refs):
            copy = pltpu.make_async_copy(ref.at[:, pl.ds(0, 3 * width)], w_s.at[a, z], sems.at[10 + 2 * a + z])
            copy.start()
            loads.append(copy)
    weights = (w_s.at[0], w_s.at[1])
    grads_a = (keep_a, send_a)
    grads_b = (keep_b, send_b)
    down_at = 2 * width
    part = rows // 2

    def vec(i):
        return vec_ref[i : i + 1, :]

    for b in range(seqs):
        for g in range(groups):
            ctx_s[b * tokens : (b + 1) * tokens, g * unit : (g + 1) * unit] = unfold(ctx_ref, b * groups + g, 0, unit)
    residual = x_ref[...].astype(F32) + dot(ctx_s[...], wo_ref[...]) + vec(1)
    centre = residual - jnp.mean(residual, -1, keepdims=True)
    scale_one = lax.rsqrt(jnp.mean(centre * centre, -1, keepdims=True) + NORM_EPSILON)
    hat = centre * scale_one
    hat_one[...] = hat
    first = hat * vec(2) + vec(3)
    first_s[...] = first.astype(BF)
    acc_s[...] = first + vec(12)
    for copy in loads:
        copy.wait()

    def place(p_rel, s_rel):
        p = jnp.bitwise_xor(core, p_rel)
        s = jnp.bitwise_xor(core, s_rel)
        return p, 2 * p + s, pl.ds(pl.multiple_of(s * width, width), width)

    units = [(p, s) for p in range(2) for s in range(2)]
    half = math.sqrt(0.5)
    for index, (p_rel, s_rel) in enumerate(units):
        p, u, columns = place(p_rel, s_rel)
        down_z = jnp.bitwise_xor(p, far)

        @pl.loop(0, rows // part)
        def _(r):
            rs = pl.ds(pl.multiple_of(r * part, part), part)
            gate = dot(first_s[rs], weights[p_rel][far, :, columns]) + vec_ref[pl.ds(4 + u, 1), :]
            up = dot(first_s[rs], weights[p_rel][1 - far, :, columns]) + vec_ref[pl.ds(8 + u, 1), :]
            cdf = 0.5 + 0.5 * lax.erf(gate * half)
            pdf = jnp.exp(gate * gate * -0.5) * (1.0 / math.sqrt(2.0 * math.pi))
            gelu = gate * cdf
            gate_s[index, rs] = up * (cdf + gate * pdf)
            up_s[index, rs] = gelu
            mixed = (gelu * up).astype(BF)
            mixed_s[index, rs] = mixed
            acc_s[rs] += dot(mixed, weights[s_rel][down_z, :, down_at : down_at + width])

    residual = acc_s[...]
    centre = residual - jnp.mean(residual, -1, keepdims=True)
    scale_two = lax.rsqrt(jnp.mean(centre * centre, -1, keepdims=True) + NORM_EPSILON)
    hat = centre * scale_two
    row = lax.broadcasted_iota(jnp.int32, (rows, 1), 0)
    valid = jnp.zeros((rows, 1), F32)
    for b in range(seqs):
        inside = (row >= b * tokens) & (row < (b + 1) * tokens) & (start + row - b * tokens < info_ref[3 + b])
        valid = jnp.where(inside, 1.0, valid)
    out_ref[...] = ((hat * vec(13) + vec(14)) * valid).astype(BF)
    grad_second = cot_ref[...].astype(F32) * valid
    gvec_ref[13:14, :] = jnp.sum(grad_second * hat, 0, keepdims=True)
    gvec_ref[14:15, :] = jnp.sum(grad_second, 0, keepdims=True)
    gvec_ref[15:16, :] = jnp.zeros((1, width), F32)
    grad_two = norm_back(grad_second, hat, scale_two, vec(13))
    acc_s[...] = grad_two
    grad_ffn = grad_two.astype(BF)
    ffn_s[...] = grad_ffn
    gvec_ref[12:13, :] = jnp.sum(grad_ffn.astype(F32), 0, keepdims=True)

    copies = []

    def write(slot, value, target, z, columns):
        if len(copies) >= 6:
            copies[len(copies) - 6].wait()
        stage[slot] = value.astype(BF)
        copy = pltpu.make_async_copy(stage.at[slot], target.at[z, :, columns], sems.at[slot])
        copy.start()
        copies.append(copy)

    for index, (p_rel, s_rel) in enumerate(units):
        p, u, columns = place(p_rel, s_rel)
        down_z = jnp.bitwise_xor(p, far)
        grad_mixed = dot(ffn_s[...], weights[s_rel][down_z, :, down_at : down_at + width], NT)
        grad_gate = (grad_mixed * gate_s[index]).astype(BF)
        grad_up = (grad_mixed * up_s[index]).astype(BF)
        ggate_s[...] = grad_gate
        gup_s[...] = grad_up
        gvec_ref[pl.ds(4 + u, 1), :] = jnp.sum(grad_gate.astype(F32), 0, keepdims=True)
        gvec_ref[pl.ds(8 + u, 1), :] = jnp.sum(grad_up.astype(F32), 0, keepdims=True)
        acc_s[...] += dot(ggate_s[...], weights[p_rel][far, :, columns], NT)
        acc_s[...] += dot(gup_s[...], weights[p_rel][1 - far, :, columns], NT)
        slot = 3 * (index % 2)
        write(slot, dot(mixed_s[index], ffn_s[...], TN), grads_b[s_rel], down_z, pl.ds(0, width))
        write(slot + 1, dot(first_s[...], ggate_s[...], TN), grads_a[p_rel], far, columns)
        write(slot + 2, dot(first_s[...], gup_s[...], TN), grads_a[p_rel], 1 - far, columns)

    grad_first = acc_s[...]
    hat = hat_one[...]
    gvec_ref[2:3, :] = jnp.sum(grad_first * hat, 0, keepdims=True)
    gvec_ref[3:4, :] = jnp.sum(grad_first, 0, keepdims=True)
    grad_one = norm_back(grad_first, hat, scale_one, vec(2))
    one_ref[...] = grad_one
    grad_att = grad_one.astype(BF)
    gvec_ref[1:2, :] = jnp.sum(grad_att.astype(F32), 0, keepdims=True)
    grad_ctx = dot(grad_att, wo_ref[...], NT).astype(BF)
    gvec_ref[0:1, :] = jnp.sum(grad_ctx.astype(F32), 0, keepdims=True)
    for b in range(seqs):
        for g in range(groups):
            fold(gctx_ref, b * groups + g, 0, grad_ctx[b * tokens : (b + 1) * tokens, g * unit : (g + 1) * unit])
    grad_wo = dot(ctx_s[...], grad_att, TN).astype(BF)
    spare = wo_s.shape[2] - width // 4
    for c in range(4):
        part = grad_wo[:, c * (width // 4) : (c + 1) * (width // 4)]
        wo_s[c] = jnp.concatenate([part, jnp.zeros((width, spare), BF)], 1)
    last = []
    for a in range(2):
        for z in range(2):
            c = 2 * jnp.bitwise_xor(far, z) + jnp.bitwise_xor(core, a)
            copy = pltpu.make_async_copy(
                wo_s.at[c],
                grads_a[a].at[z, :, pl.ds(2 * width, wo_s.shape[2])],
                sems.at[6 + 2 * a + z],
            )
            copy.start()
            last.append(copy)
    for copy in copies[-6:] + last:
        copy.wait()


def feed_forward(info, vec, x, ctx, cot, wo, weights, groups):
    rows, width = x.shape
    vmem = pl.BlockSpec(memory_space=pltpu.VMEM)
    smem = pl.BlockSpec(memory_space=pltpu.SMEM)
    hbm = pl.BlockSpec(memory_space=pl.ANY)
    grads_a = jax.ShapeDtypeStruct((2, width, 2 * width + 256), BF)
    grads_b = jax.ShapeDtypeStruct((2, width, width), BF)
    return pl.pallas_call(
        functools.partial(feed_forward_kernel, groups),
        out_shape=(
            jax.ShapeDtypeStruct((rows, width), BF),
            jax.ShapeDtypeStruct((rows, width), F32),
            jax.ShapeDtypeStruct(ctx.shape, BF),
            jax.ShapeDtypeStruct((16, width), F32),
            grads_a,
            grads_a,
            grads_b,
            grads_b,
        ),
        in_specs=[smem] + [vmem] * 5 + [hbm] * 4,
        out_specs=(vmem,) * 4 + (hbm,) * 4,
        scratch_shapes=[
            pltpu.VMEM((2, 2, width, 3 * width), BF),
            pltpu.VMEM((rows, width), BF),
            pltpu.VMEM((rows, width), F32),
            pltpu.VMEM((rows, width), BF),
            pltpu.VMEM((rows, width), F32),
            pltpu.VMEM((4, rows, width), F32),
            pltpu.VMEM((4, rows, width), F32),
            pltpu.VMEM((6, width, width), BF),
            pltpu.VMEM((4, width, 256), BF),
            pltpu.VMEM((rows, width), BF),
            pltpu.VMEM((4, rows, width), BF),
            pltpu.VMEM((rows, width), BF),
            pltpu.VMEM((rows, width), BF),
            pltpu.SemaphoreType.DMA((14,)),
        ],
        compiler_params=pltpu.CompilerParams(vmem_limit_bytes=VMEM_LIMIT),
        cost_estimate=pl.CostEstimate(
            flops=60 * rows * width * width, bytes_accessed=34_000_000, transcendentals=0
        ),
        name="feed_forward",
    )(info, vec, x, ctx, cot, wo, *weights)


def qkv_grad_kernel(groups, heads, info_ref, x_ref, *refs):
    grad_refs = refs[:heads]
    rows_ref, keep_ref, send_ref, w_s = refs[-4:]
    core = info_ref[0]
    tokens = rows_ref.shape[1]
    seqs = rows_ref.shape[0] // groups
    unit = w_s.shape[2]
    for g in range(groups):
        total = None
        for b in range(seqs):
            owner = b * groups + g
            for role in range(3):
                for h in range(heads):
                    at = role * unit + h * HEAD_DIM
                    rows_ref[owner, :, at : at + HEAD_DIM] = unfold(grad_refs[h], owner, role * HEAD_DIM, HEAD_DIM)
            grads = rows_ref[owner]
            part = dot(x_ref[b * tokens : (b + 1) * tokens, :], grads, TN)
            total = part if total is None else total + part
        for role in range(3):
            w_s[role * groups + g] = total[:, role * unit : (role + 1) * unit].astype(BF)
    for a, ref in enumerate((keep_ref, send_ref)):
        for z in range(2):
            c = 2 * z + jnp.bitwise_xor(core, a)
            for i in range(3):
                at = (3 * z + i) * unit
                ref[:, at : at + unit] = w_s[3 * c + i]


def qkv_grad(info, x, grads, groups, *others):
    rows, width = x.shape
    heads = len(grads)
    unit = heads * HEAD_DIM
    vmem = pl.BlockSpec(memory_space=pltpu.VMEM)
    smem = pl.BlockSpec(memory_space=pltpu.SMEM)
    out = jax.ShapeDtypeStruct((width, 6 * unit), BF)
    return pl.pallas_call(
        functools.partial(qkv_grad_kernel, groups, heads),
        out_shape=(
            jax.ShapeDtypeStruct((grads[0].shape[0], 2 * grads[0].shape[1], 3 * unit), BF),
            out,
            out,
        ),
        in_specs=[smem] + [vmem] * (1 + heads) + [pl.BlockSpec(memory_space=pl.ANY)] * len(others),
        out_specs=(vmem,) * 3,
        scratch_shapes=[pltpu.VMEM((12, width, unit), BF)],
        compiler_params=pltpu.CompilerParams(vmem_limit_bytes=VMEM_LIMIT),
        cost_estimate=pl.CostEstimate(
            flops=6 * rows * width * width, bytes_accessed=9_000_000, transcendentals=0
        ),
        name="qkv_grad",
    )(info, x, *grads, *others)


def input_grad_kernel(groups, one_ref, grad_ref, group_ref, *rest):
    out_ref = rest[-1]
    tokens = grad_ref.shape[1]
    for b in range(grad_ref.shape[0] // groups):
        total = one_ref[b * tokens : (b + 1) * tokens, :]
        for g in range(groups):
            total = total + dot(grad_ref[b * groups + g], group_ref[g], NT)
        out_ref[b * tokens : (b + 1) * tokens, :] = total.astype(BF)


def input_grad(grad_one, grads, group, groups, *others):
    rows, width = grad_one.shape
    vmem = pl.BlockSpec(memory_space=pltpu.VMEM)
    return pl.pallas_call(
        functools.partial(input_grad_kernel, groups),
        out_shape=jax.ShapeDtypeStruct((rows, width), BF),
        in_specs=[vmem] * 3 + [pl.BlockSpec(memory_space=pl.ANY)] * len(others),
        out_specs=vmem,
        compiler_params=pltpu.CompilerParams(vmem_limit_bytes=VMEM_LIMIT),
        cost_estimate=pl.CostEstimate(
            flops=6 * rows * width * width, bytes_accessed=8_000_000, transcendentals=0
        ),
        name="input_grad",
    )(grad_one, grads, group, *others)


def on_device(
    hidden_in,
    cotangent,
    lengths,
    w_qkv,
    w_out,
    w_gated,
    w_down,
    vectors,
    mom_qkv,
    mom_out,
    mom_gated,
    mom_down,
    vec_first,
    vec_second,
):
    seqs, tokens, width = hidden_in.shape
    seq_count = lax.axis_size("seq")
    head_count = lax.axis_size("head")
    n = seq_count * head_count
    bits = n.bit_length() - 1
    length = tokens * n
    d = lax.axis_index("dp")
    seq_index = lax.axis_index("seq")
    head_index = lax.axis_index("head")
    j = seq_index * head_count + head_index
    core = lax.rem(d, 2)
    far = d // 2
    cols = w_qkv.shape[1]
    piece_rows = width // n

    def swap(value, over_dp=0, over_group=0):
        pairs = [
            (a * n + b, (a ^ over_dp) * n + (b ^ over_group)) for a in range(4) for b in range(n)
        ]
        return lax.ppermute(value, AXES, pairs)

    def bit_of(k):
        return lax.rem(j // (2**k), 2)

    def pick(value, index, axis=0):
        return lax.dynamic_index_in_dim(value, index, axis, keepdims=False)

    def join(cur, k, axis):
        other = swap(cur, 0, 2**k)
        first = bit_of(k) == 0
        return jnp.concatenate([jnp.where(first, cur, other), jnp.where(first, other, cur)], axis)

    def gather_group(piece, order):
        cur = piece.reshape((1,) * bits + piece.shape)
        for k in order:
            cur = join(cur, k, bits - 1 - k)
        return cur.reshape((n * piece.shape[0],) + piece.shape[1:])

    head_bits = head_count.bit_length() - 1

    def gather_rows(piece, axis):
        for k in range(head_bits):
            piece = join(piece, k, axis)
        return lax.all_gather(piece, "seq", axis=axis, tiled=True)

    def halve(value, k, axis):
        return pick(value, bit_of(k), axis), pick(value, 1 - bit_of(k), axis)

    def add(kept, got):
        return (kept.astype(F32) + got.astype(F32)).astype(BF)

    def rows_of(value):
        return lax.dynamic_slice_in_dim(value, j * piece_rows, piece_rows, 0)

    piece = swap(jnp.concatenate([rows_of(w_qkv), rows_of(w_out)], 1).astype(BF), 2)
    own_qo = jnp.concatenate([w_qkv, w_out], 1).astype(BF)
    rest_rows = width // seq_count

    def seq_rows(value):
        return lax.dynamic_slice_in_dim(value, seq_index * rest_rows, rest_rows, 0)

    rest = jnp.concatenate([seq_rows(w_gated), seq_rows(w_down)], 1).astype(BF)
    piece = after(piece, rest)
    rest = swap(rest, 2)
    own_rest = jnp.concatenate([w_gated.astype(BF), w_down.astype(BF)], 1)
    own_qo_two = swap(own_qo, 1)
    far_qo = gather_group(piece, range(bits))
    far_qo_two = swap(far_qo, 1)

    vec_low = vectors.astype(BF)
    vec_rel = [vec_low] + [swap(vec_low, k) for k in (1, 2, 3)]
    vec_pair = [
        jnp.where(core == 0, jnp.stack([vec_rel[a], vec_rel[a + 1]]), jnp.stack([vec_rel[a + 1], vec_rel[a]]))
        for a in (0, 2)
    ]
    vec = jnp.concatenate(
        [jnp.where(far == 0, vec_pair[0], vec_pair[1]), jnp.where(far == 0, vec_pair[1], vec_pair[0])]
    ).reshape(-1, width)
    vec = jnp.concatenate([vec.astype(F32), jnp.zeros((1, width), F32)])

    inner = math.gcd(n, seqs * HEADS)
    heads = seqs * HEADS // inner
    groups = inner // seqs
    unit = heads * HEAD_DIM
    me = lax.rem(j, inner)

    def exchange(blocks):
        if n == inner:
            return lax.all_to_all(blocks, ("seq", "head"), 0, 0, tiled=True)
        got = []
        for r in range(inner):
            block = pick(blocks, jnp.bitwise_xor(me, r))
            got.append(block if r == 0 else swap(block, 0, r))
        return jnp.take(jnp.stack(got), jnp.bitwise_xor(jnp.arange(inner), me), axis=0)

    info = jnp.concatenate([jnp.stack([core, far, j * tokens]), lengths]).astype(jnp.int32)
    x = hidden_in.reshape(seqs * tokens, width)
    owned, group_w, w_o = project(info, vec, x, (own_qo, far_qo, own_qo_two, far_qo_two), groups, tokens)
    own_rest_two = swap(own_rest, 1)
    qkv = exchange(owned)
    far_rest = lax.all_gather(after(rest, far_qo), "seq", axis=0, tiled=True)
    if n > inner:
        qkv = jnp.concatenate([qkv] + [swap(qkv, 0, s * inner) for s in range(1, n // inner)], 0)
    first_head = lax.rem(me, groups) * heads
    place = jnp.stack([j - me, pick(lengths, me // groups)]).astype(jnp.int32)
    head_ids = (first_head + jnp.arange(heads)).astype(F32)
    slopes = jnp.exp2(-8.0 * (head_ids + 1.0) / HEADS) * (64.0 / length)
    attention, attention_low, log_total = attention_forward(place, slopes, qkv, tokens, inner)
    context = exchange(attention_low)
    far_rest = after(far_rest, attention_low)
    far_rest_two = swap(far_rest, 1)
    hidden_out, grad_one, grad_context, grad_vec, keep_a, send_a, keep_b, send_b = feed_forward(
        info,
        vec,
        x,
        context,
        cotangent.reshape(seqs * tokens, width),
        w_o,
        (own_rest, far_rest, own_rest_two, far_rest_two),
        groups,
    )
    grad_owned = exchange(grad_context)

    third = keep_a.shape[2] // 2
    orders = [[(k + i) % bits for k in range(bits)] for i in (1, 2, 0)]
    bit_values = jnp.stack([bit_of(k) for k in range(bits)]).astype(jnp.int32)

    def by_bits(value):
        return value.reshape((2,) + (2,) * bits + (piece_rows, value.shape[2]))

    grad_vector = grad_vec[:15].reshape(2, 2, -1)
    vector = pick(grad_vector, core, 1), swap(pick(grad_vector, 1 - core, 1), 1)
    pairs = [(by_bits(keep_a), by_bits(swap(send_a, 1))), (by_bits(keep_b), by_bits(swap(send_b, 1)))]
    spans = [(0, 0, third), (0, third, 2 * third), (1, 0, keep_b.shape[2])]

    def split_step(step, pairs, spans, vector, *waits):
        if step < bits:
            places = [span + (bits - order[step], order[step]) for span, order in zip(spans, orders)]
        else:
            places = [span + (0, None) for span in spans]
        *values, vector = sum_split(places, bit_values, pairs, vector, waits)
        if step == bits:
            return values[::2], values[1::2], vector
        values = [
            value.reshape(value.shape[:place[3]] + (1,) + value.shape[place[3] :])
            for value, place in zip(values, [p for p in places for i in range(2)])
        ]
        got = [swap(value, 0, 2 ** order[step]) for value, order in zip(values[1::2], orders)]
        return list(zip(values[::2], got)), values[1::2], vector

    def backward(head, *others):
        return attention_backward(
            head, place, slopes, qkv, attention, log_total, grad_owned, tokens, inner, *others
        )

    def finish(grads):
        if n > inner:
            total = grads[:inner]
            for s in range(1, n // inner):
                total = total + swap(grads[s * inner : (s + 1) * inner], 0, s * inner)
            grads = total.astype(BF)
        return exchange(grads)

    def own_momentum():
        gated = rows_of(mom_gated)
        out = rows_of(mom_out)
        spare = jnp.zeros((piece_rows, 2 * third - gated.shape[1] - out.shape[1]), F32)
        return gated[:, :third], jnp.concatenate([gated[:, third:], out, spare], 1), rows_of(mom_down)

    old = own_momentum()
    head_rows = []
    waits = []
    for step in range(max(heads, bits)):
        if step < bits:
            pairs, sent, total = split_step(step, pairs, spans, vector, *waits)
            spans = [(i, 0, pair[0].shape[-1]) for i, pair in enumerate(pairs)]
            vector = total, swap(total, 0, 2**step)
            waits = [*sent, total]
        if step < heads:
            if step == heads - 1:
                waits.append(head_rows[0])
            back = backward(step, *waits)
            if step < heads - 1:
                head_rows.append(finish(back))
            waits = [back]
    own_parts, far_parts, total = split_step(bits, pairs, spans, vector, back)
    head_rows.append(finish(after(back, *far_parts)))
    parts = [
        (MUON_BETA * m + value.reshape(m.shape).astype(F32) + swap(other.reshape(m.shape), 2).astype(F32)).astype(BF)
        for m, value, other in zip(old, own_parts, far_parts)
    ]
    summed_vector = pick(total, far) + swap(pick(total, 1 - far), 2)

    def gather_parts(parts, step, *wait):
        others = [swap(part, 0, 2 ** order[step]) for part, order in zip(parts, orders)]
        places = [(bits - 1 - order[step], order[step]) for order in orders]
        return join_pairs(places, bit_values, parts, others, wait)

    shards = [part.reshape((1,) * bits + part.shape) for part in parts]

    grad_rows, keep, send = qkv_grad(info, x, head_rows, groups, *parts, summed_vector)
    shards = gather_parts(shards, 0, send)
    sum_qkv = add(keep, swap(send, 1))
    shards = gather_parts(shards, 1, sum_qkv)
    grad_in = input_grad(grad_one, grad_rows, group_w, groups, sum_qkv, *shards)
    sum_qkv = after(lax.psum_scatter(sum_qkv, "seq", scatter_dimension=0, tiled=True), grad_in)
    for step in range(2, bits):
        shards = gather_parts(shards, step, grad_in)
    shards = [part.reshape(width, part.shape[-1]) for part in shards]
    grad_in = grad_in.reshape(seqs, tokens, width)
    for k in reversed(range(head_bits)):
        kept, send = halve(sum_qkv.reshape(2, sum_qkv.shape[0] // 2, 2 * cols), k, 0)
        sum_qkv = add(kept, swap(send, 0, 2**k))
    old = MUON_BETA * rows_of(mom_qkv)
    near = far == 0
    old = jnp.concatenate([jnp.where(near, old, 0.0), jnp.where(near, 0.0, old)], 1)
    sum_qkv = (sum_qkv.astype(F32) + old).astype(BF)
    far_sum = swap(sum_qkv, 2)

    full_shapes = ((D, 3 * D), (D, D), (D, 2 * FF), (FF, D))
    factors = [MUON_RATE * 0.2 * math.sqrt(max(shape)) for shape in full_shapes]

    stride = seq_count // 4
    which = seq_index // stride
    kind = which.reshape(1).astype(jnp.int32)
    gated_at = w_gated.shape[1] - third
    out_at = gated_at + w_out.shape[1]
    packed = upper_gram(kind, *shards, w_gated.shape[1], w_out.shape[1])
    mine_m = gather_rows(add(sum_qkv, after(far_sum, packed)), 0)
    new_gated = jnp.concatenate([shards[0], shards[1][:, :gated_at]], 1).astype(F32)
    new_out = shards[1][:, gated_at:out_at].astype(F32)
    new_down = shards[2].astype(F32)
    count = len(PAIRS) // head_count
    part = lax.dynamic_slice_in_dim(packed, head_index * count, count, 1)
    part = pick(part, core) + swap(pick(part, 1 - core), 1)
    part = part + after(swap(part, 2), new_gated, new_down)
    theirs_m = swap(mine_m, 1)
    for k in range(head_bits):
        part = join(part, k, 0)
    other_core = swap(part, 1)
    packed = jnp.stack([jnp.where(core == 0, part, other_core), jnp.where(core == 0, other_core, part)])

    low_qkv = jnp.where(near, mine_m[:, :cols], mine_m[:, cols:])
    new_qkv = low_qkv.astype(F32)
    factor = newton_schulz(kind, packed, mine_m, theirs_m, 3, low_qkv)

    half_factor = pick(factor.reshape(2, width // 2, width), core)
    halves = [half_factor] + [swap(half_factor, 0, k * stride * head_count) for k in (1, 2, 3)]
    others = [swap(value, 1) for value in halves]
    new_w_gated, new_w_down, new_w_out, new_w_qkv = update(
        (factors[2], factors[3], factors[1], factors[0]),
        jnp.stack([which, core]).astype(jnp.int32),
        halves,
        others,
        (*shards, low_qkv),
        (w_gated, w_down, w_out.T, w_qkv.T),
    )
    moments = (new_qkv, new_out, new_gated, new_down)
    new_weights = (new_w_qkv.T, new_w_out.T, new_w_gated, new_w_down)
    first_new = ADAM_BETA_ONE * vec_first + (1.0 - ADAM_BETA_ONE) * summed_vector
    second_new = ADAM_BETA_TWO * vec_second + (1.0 - ADAM_BETA_TWO) * summed_vector * summed_vector
    first_hat = first_new / (1.0 - ADAM_BETA_ONE**STEP)
    second_hat = second_new / (1.0 - ADAM_BETA_TWO**STEP)
    vectors_new = vectors - ADAM_RATE * first_hat / (jnp.sqrt(second_hat) + ADAM_EPSILON)
    hidden_out = hidden_out.reshape(seqs, tokens, width)
    return (hidden_out, grad_in) + moments + new_weights + (first_new, second_new, vectors_new)


def solution(mesh):
    tokens = P("dp", ("seq", "head"), None)
    wide = P(None, "dp")
    tall = P("dp", None)
    flat = P("dp")
    in_specs = (tokens, tokens, flat) + (wide, wide, wide, tall, flat) + (wide, wide, wide, tall, flat, flat)
    out_specs = (tokens, tokens) + (wide, wide, wide, tall) * 2 + (flat, flat, flat)
    return jax.shard_map(on_device, mesh=mesh, in_specs=in_specs, out_specs=out_specs, check_vma=False)
```

```python
import functools
import math

import jax
import jax.numpy as jnp
from jax import lax
from jax.experimental import pallas as pl
from jax.experimental.pallas import tpu as pltpu
from jax.sharding import PartitionSpec as P

D = 768
HEADS = 12
HEAD_DIM = 64
FF = 3072
NS_STEPS = 5
STEP = 10

POLY_A = 3.4445
POLY_B = -4.775
POLY_C = 2.0315
MUON_BETA = 0.95
MUON_RATE = 0.3
MUON_DECAY = 0.01
ADAM_BETA_ONE = 0.9
ADAM_BETA_TWO = 0.999
ADAM_RATE = 0.4
ADAM_EPSILON = 1e-08
NORM_EPSILON = 1e-06
MASKED = -1e30

BF = jnp.bfloat16
F32 = jnp.float32
AXES = ("dp", "seq", "head")
VMEM_LIMIT = 60 * 1024 * 1024
NT = (((1,), (1,)), ((), ()))
NN = (((1,), (0,)), ((), ()))
TN = (((0,), (0,)), ((), ()))


def dot(a, b, dims=NN):
    return lax.dot_general(a, b, dims, preferred_element_type=F32)


def split_three(value):
    high = value.astype(BF)
    rest = value - high.astype(F32)
    mid = rest.astype(BF)
    low = (rest - mid.astype(F32)).astype(BF)
    return high.astype(F32), mid.astype(F32), low.astype(F32)


def after(value, *others):
    hbm = pl.BlockSpec(memory_space=pl.ANY)
    return pl.pallas_call(
        lambda *refs: None,
        out_shape=jax.ShapeDtypeStruct(value.shape, value.dtype),
        in_specs=[hbm] * (1 + len(others)),
        out_specs=hbm,
        input_output_aliases={0: 0},
        name="after",
    )(value, *others)


def unfold(ref, block, at, count):
    columns = ref.shape[2] // 2
    return jnp.concatenate([ref[block, :, at : at + count], ref[block, :, columns + at : columns + at + count]], 0)


def fold(ref, block, at, value):
    columns = ref.shape[2] // 2
    half = value.shape[0] // 2
    count = value.shape[1]
    ref[block, :, at : at + count] = value[:half].astype(ref.dtype)
    ref[block, :, columns + at : columns + at + count] = value[half:].astype(ref.dtype)


def sum_split_kernel(places, pairs, with_vector, bits_ref, *refs):
    ins = refs[: 2 * pairs]
    vector = refs[2 * pairs : 2 * pairs + 2]
    outs = refs[len(refs) - 2 * len(places) - with_vector :]
    for place, (pair, low, high, axis, which) in enumerate(places):
        mine = 0 if which is None else bits_ref[which]
        for other, out in enumerate(outs[2 * place : 2 * place + 2]):
            at = mine if other == 0 else 1 - mine
            index = (slice(None),) * axis + (at, Ellipsis, slice(low, high))
            first, second = ins[2 * pair], ins[2 * pair + 1]
            out[...] = (first[index].astype(F32) + second[index].astype(F32)).astype(BF)
    if with_vector:
        outs[-1][...] = vector[0][...] + vector[1][...]


def sum_split(places, bits, pairs, vector=None, waits=()):
    smem = pl.BlockSpec(memory_space=pltpu.SMEM)
    by_half = min(place[3] for place in places) > 0
    arrays = [array for pair in pairs for array in pair]
    shapes = []
    for pair, low, high, axis, which in places:
        shape = pairs[pair][0].shape
        shape = shape[:axis] + shape[axis + 1 : -1] + (high - low,)
        shapes += [jax.ShapeDtypeStruct(shape, BF)] * 2

    def spec(array):
        if by_half:
            return pl.BlockSpec((1,) + array.shape[1:], lambda z: (z,) + (0,) * (len(array.shape) - 1))
        return pl.BlockSpec(memory_space=pltpu.VMEM)

    def whole(array):
        if by_half:
            return pl.BlockSpec(array.shape, lambda z: (0,) * len(array.shape))
        return pl.BlockSpec(memory_space=pltpu.VMEM)

    in_specs = [smem] + [spec(array) for array in arrays]
    out_specs = [spec(shape) for shape in shapes]
    if vector:
        arrays += list(vector)
        in_specs += [whole(vector[0])] * 2
        shapes.append(jax.ShapeDtypeStruct(vector[0].shape, F32))
        out_specs.append(whole(vector[0]))
    return pl.pallas_call(
        functools.partial(sum_split_kernel, places, len(pairs), 1 if vector else 0),
        grid=(2,) if by_half else (),
        out_shape=tuple(shapes),
        in_specs=in_specs + [pl.BlockSpec(memory_space=pl.ANY)] * len(waits),
        out_specs=tuple(out_specs),
        compiler_params=pltpu.CompilerParams(vmem_limit_bytes=VMEM_LIMIT),
        cost_estimate=pl.CostEstimate(
            flops=0, bytes_accessed=sum(3 * 2 * p[0].size for p in pairs), transcendentals=0
        ),
        name="sum_split",
    )(bits, *arrays, *waits)


def join_kernel(places, bits_ref, *refs):
    count = len(places)
    outs = refs[-count:]
    for index, (axis, which) in enumerate(places):
        before = (slice(None),) * axis
        mine = bits_ref[which]
        outs[index][before + (mine,)] = refs[index][before + (0,)]
        outs[index][before + (1 - mine,)] = refs[count + index][before + (0,)]


def join_pairs(places, bits, mine, others, waits=()):
    vmem = pl.BlockSpec(memory_space=pltpu.VMEM)
    smem = pl.BlockSpec(memory_space=pltpu.SMEM)
    shapes = tuple(
        jax.ShapeDtypeStruct(array.shape[:axis] + (2,) + array.shape[axis + 1 :], array.dtype)
        for array, (axis, which) in zip(mine, places)
    )
    return pl.pallas_call(
        functools.partial(join_kernel, places),
        out_shape=shapes,
        in_specs=[smem] + [vmem] * (2 * len(mine)) + [pl.BlockSpec(memory_space=pl.ANY)] * len(waits),
        out_specs=(vmem,) * len(mine),
        compiler_params=pltpu.CompilerParams(vmem_limit_bytes=VMEM_LIMIT),
        cost_estimate=pl.CostEstimate(
            flops=0, bytes_accessed=sum(8 * array.size for array in mine), transcendentals=0
        ),
        name="join_pairs",
    )(bits, *mine, *others, *waits)


def key_features(keys, start, rows, length):
    lane = lax.broadcasted_iota(jnp.int32, (rows, 128), 1)
    pos = start + lax.broadcasted_iota(jnp.int32, (rows, 128), 0)
    low = jnp.bitwise_and(pos, 255)
    feats = jnp.where(lane < 68, (pos - low).astype(F32), jnp.where(lane < 71, low.astype(F32), 1.0))
    feats = jnp.where(lane == 64, jnp.where(pos >= length, MASKED, 0.0), feats)
    wide = jnp.concatenate([keys.astype(F32), jnp.zeros_like(keys, F32)], 1)
    return jnp.where(lane < 64, wide, jnp.where(lane < 77, feats, 0.0))


def query_features(queries, start, rows, slope, log_total):
    lane = lax.broadcasted_iota(jnp.int32, (rows, 128), 1)
    first = lax.broadcasted_iota(jnp.int32, (1, 128), 1)
    pos = (start + lax.broadcasted_iota(jnp.int32, (rows, 128), 0)).astype(F32)
    tilt = jnp.zeros((1, 128), F32)
    for offset, piece in enumerate(split_three(jnp.full((1, 128), slope, F32))):
        tilt = jnp.where((first == 65 + offset) | (first == 68 + offset), -piece, tilt)
    tilt = jnp.broadcast_to(tilt, (rows, 128))
    for offset, piece in enumerate(split_three(pos * slope)):
        tilt = jnp.where(lane == 71 + offset, piece, tilt)
    base = jnp.concatenate([queries.astype(F32) * (1.0 / math.sqrt(HEAD_DIM)), jnp.zeros_like(queries, F32)], 1)
    base = jnp.where(lane == 64, 1.0, base)
    if log_total is not None:
        for offset, piece in enumerate(split_three(log_total)):
            base = jnp.where(lane == 74 + offset, -piece, base)
    return base, tilt


def distances(slope, rows):
    row = lax.broadcasted_iota(jnp.int32, (2 * rows, rows), 0)
    col = lax.broadcasted_iota(jnp.int32, (2 * rows, rows), 1)
    first = jnp.abs(row - col).astype(F32) * slope
    second = jnp.abs(row - col - rows).astype(F32) * slope
    return jnp.zeros_like(first), first, second


def relation(pair, block, mine):
    start = jnp.bitwise_xor(2 * pair, mine)
    other = jnp.bitwise_xor(block, mine)
    behind = jnp.where(start > other, 1, 0)
    before = jnp.where(start + 1 < other, 1, 0)
    return jnp.where(behind + before == 0, 1 + other - start, 0), behind - before


def with_ones(values, count):
    rows = values.shape[0]
    lane = lax.broadcasted_iota(jnp.int32, (rows, 128), 1)
    wide = jnp.concatenate([values.astype(F32), jnp.zeros_like(values, F32)], 1)
    return jnp.where(lane < 64, wide, jnp.where(lane < 64 + count, 1.0, 0.0)).astype(BF)


def attention_forward_kernel(
    rows, q_blocks, k_blocks, heads, info_ref, slope_ref, qkv_ref, out_ref, low_ref, log_ref, q_s, k_s, v_s, t_s, o_s
):
    mine = info_ref[0]
    length = info_ref[1]
    narrow = heads * HEAD_DIM
    for h in range(heads):
        lo = h * HEAD_DIM

        @pl.loop(0, k_blocks)
        def _(r):
            rs = pl.ds(pl.multiple_of(r * rows, rows), rows)
            start = jnp.bitwise_xor(r, mine) * rows
            keys = key_features(unfold(qkv_ref, r, narrow + lo, HEAD_DIM), start, rows, length)
            k_s[h, r] = keys.T.astype(BF)
            v_s[h, rs] = with_ones(unfold(qkv_ref, r, 2 * narrow + lo, HEAD_DIM), 1)

        @pl.loop(0, q_blocks)
        def _(r):
            rs = pl.ds(pl.multiple_of(r * rows, rows), rows)
            start = jnp.bitwise_xor(r, mine) * rows
            queries = unfold(qkv_ref, r, lo, HEAD_DIM)
            base, tilt = query_features(queries, start, rows, slope_ref[h], None)
            q_s[h, 0, rs] = (base - tilt).astype(BF)
            q_s[h, 1, rs] = base.astype(BF)
            q_s[h, 2, rs] = (base + tilt).astype(BF)

        for index, value in enumerate(distances(slope_ref[h], rows)):
            t_s[h, index] = value

    wide = 2 * rows

    def attend(h, pair):
        rs = pl.ds(pl.multiple_of(pair * wide, wide), wide)
        scores = []
        for kb in range(k_blocks):
            index, side = relation(pair, kb, mine)
            scores.append(dot(q_s[h, 1 - side, rs], k_s[h, kb]) - t_s[h, index])
        high = scores[0]
        for s in scores[1:]:
            high = jnp.maximum(high, s)
        high = jnp.max(high, -1, keepdims=True)
        weights = jnp.concatenate([jnp.exp(s - high).astype(BF) for s in scores], 1)
        total = dot(weights, v_s[h])
        norm = total[:, HEAD_DIM : HEAD_DIM + 1]
        return total[:, :HEAD_DIM] / norm, high + jnp.log(norm)

    lane = lax.broadcasted_iota(jnp.int32, (wide, 128), 1)
    if q_blocks == k_blocks:

        @pl.loop(0, q_blocks // 2)
        def _(pair):
            rs = pl.ds(pl.multiple_of(pair * wide, wide), wide)
            results = [attend(h, pair) for h in range(heads)]
            logs = jnp.zeros((wide, 128), F32)
            for h, (value, log) in enumerate(results):
                o_s[h, rs] = value
                logs = jnp.where(lane == h, log, logs)
            log_ref[rs] = logs

    else:
        log_ref[...] = jnp.zeros_like(log_ref)

        @pl.loop(0, heads * q_blocks // 2)
        def _(step):
            h = step // (q_blocks // 2)
            pair = lax.rem(step, q_blocks // 2)
            rs = pl.ds(pl.multiple_of(pair * wide, wide), wide)
            value, log = attend(h, pair)
            o_s[h, rs] = value
            log_ref[rs] = jnp.where(lane == h, log, log_ref[rs])

    for h in range(heads):
        out_ref[:, h * HEAD_DIM : (h + 1) * HEAD_DIM] = o_s[h]
        for r in range(q_blocks):
            fold(low_ref, r, h * HEAD_DIM, o_s[h, r * rows : (r + 1) * rows])


def attention_forward(info, slopes, qkv, rows, q_blocks):
    heads = qkv.shape[2] // (6 * HEAD_DIM)
    k_blocks = qkv.shape[0]
    q_rows = q_blocks * rows
    vmem = pl.BlockSpec(memory_space=pltpu.VMEM)
    smem = pl.BlockSpec(memory_space=pltpu.SMEM)
    return pl.pallas_call(
        functools.partial(attention_forward_kernel, rows, q_blocks, k_blocks, heads),
        out_shape=(
            jax.ShapeDtypeStruct((q_rows, heads * HEAD_DIM), F32),
            jax.ShapeDtypeStruct((q_blocks, rows // 2, 2 * heads * HEAD_DIM), BF),
            jax.ShapeDtypeStruct((q_rows, 128), F32),
        ),
        in_specs=[smem, smem, vmem],
        out_specs=(vmem, vmem, vmem),
        scratch_shapes=[
            pltpu.VMEM((heads, 3, q_rows, 128), BF),
            pltpu.VMEM((heads, k_blocks, 128, rows), BF),
            pltpu.VMEM((heads, k_blocks * rows, 128), BF),
            pltpu.VMEM((heads, 3, 2 * rows, rows), F32),
            pltpu.VMEM((heads, q_rows, HEAD_DIM), F32),
        ],
        compiler_params=pltpu.CompilerParams(vmem_limit_bytes=VMEM_LIMIT),
        cost_estimate=pl.CostEstimate(
            flops=16 * heads * q_rows * k_blocks * rows * HEAD_DIM, bytes_accessed=6_000_000, transcendentals=0
        ),
        name="attention_forward",
    )(info, slopes, qkv)


def attention_backward_kernel(
    rows,
    q_blocks,
    k_blocks,
    heads,
    head,
    info_ref,
    slope_ref,
    qkv_ref,
    att_ref,
    log_ref,
    grad_ref,
    *rest,
):
    out_ref, q_s, qt_s, k_s, v_s, g_s, gt_s, t_s, kt_s, dq_s, dk_s, dv_s = rest[-12:]
    mine = info_ref[0]
    length = info_ref[1]
    narrow = heads * HEAD_DIM
    scale = 1.0 / math.sqrt(HEAD_DIM)
    lo = head * HEAD_DIM
    slope = slope_ref[head]

    @pl.loop(0, k_blocks)
    def _(r):
        rs = pl.ds(pl.multiple_of(r * rows, rows), rows)
        start = jnp.bitwise_xor(r, mine) * rows
        keys = unfold(qkv_ref, r, narrow + lo, HEAD_DIM)
        k_s[rs] = key_features(keys, start, rows, length).astype(BF)
        kt_s[r // 2, lax.rem(r, 2)] = keys.astype(F32).T.astype(BF)
        v_s[rs] = with_ones(unfold(qkv_ref, r, 2 * narrow + lo, HEAD_DIM), 3)

    @pl.loop(0, q_blocks)
    def _(r):
        rs = pl.ds(pl.multiple_of(r * rows, rows), rows)
        start = jnp.bitwise_xor(r, mine) * rows
        queries = unfold(qkv_ref, r, lo, HEAD_DIM)
        log_total = log_ref[rs, head : head + 1]
        base, tilt = query_features(queries, start, rows, slope, log_total)
        q_s[rs] = base.astype(BF)
        base = base.T
        tilt = tilt.T
        qt_s[0, r] = (base - tilt).astype(BF)
        qt_s[1, r] = base.astype(BF)
        qt_s[2, r] = (base + tilt).astype(BF)
        grads = unfold(grad_ref, r, lo, HEAD_DIM).astype(F32)
        delta = jnp.sum(grads * att_ref[rs, lo : lo + HEAD_DIM], -1, keepdims=True)
        lane = lax.broadcasted_iota(jnp.int32, (rows, 128), 1)
        wide = jnp.concatenate([grads, jnp.zeros_like(grads)], 1)
        for offset, piece in zip((64, 65, 66), split_three(delta)):
            wide = jnp.where(lane == offset, -piece, wide)
        g_s[rs] = wide.astype(BF)
        gt_s[r] = wide.T.astype(BF)

    for index, value in enumerate(distances(slope, rows)):
        t_s[index] = value
    dq_s[...] = jnp.zeros_like(dq_s)
    wide = 2 * rows

    @pl.loop(0, k_blocks // 2)
    def _(pair):
        ks = pl.ds(pl.multiple_of(pair * wide, wide), wide)
        keys = k_s[ks]
        values = v_s[ks]
        weights, grad_scores = [], []
        for qb in range(q_blocks):
            index, side = relation(pair, qb, mine)
            w = jnp.exp(dot(keys, qt_s[1 + side, qb]) - t_s[index])
            grad_scores.append((w * dot(values, gt_s[qb])).astype(BF))
            weights.append(w.astype(BF))
        grad_scores = jnp.concatenate(grad_scores, 1)
        dv_s[ks] = dot(jnp.concatenate(weights, 1), g_s[...])[:, :HEAD_DIM]
        dk_s[ks] = dot(grad_scores, q_s[...])[:, :HEAD_DIM]
        dq_s[...] += dot(jnp.concatenate([kt_s[pair, 0], kt_s[pair, 1]], 1), grad_scores)

    for r in range(k_blocks):
        rs = slice(r * rows, (r + 1) * rows)
        if r < q_blocks:
            fold(out_ref, r, 0, dq_s[:, rs].T * scale)
        else:
            fold(out_ref, r, 0, jnp.zeros((rows, HEAD_DIM), F32))
        fold(out_ref, r, HEAD_DIM, dk_s[rs])
        fold(out_ref, r, 2 * HEAD_DIM, dv_s[rs])


def attention_backward(head, info, slopes, qkv, attention, log_total, grads, rows, q_blocks, *others):
    heads = qkv.shape[2] // (6 * HEAD_DIM)
    k_blocks = qkv.shape[0]
    q_rows = q_blocks * rows
    k_rows = k_blocks * rows
    vmem = pl.BlockSpec(memory_space=pltpu.VMEM)
    smem = pl.BlockSpec(memory_space=pltpu.SMEM)
    hbm = pl.BlockSpec(memory_space=pl.ANY)
    return pl.pallas_call(
        functools.partial(attention_backward_kernel, rows, q_blocks, k_blocks, heads, head),
        out_shape=jax.ShapeDtypeStruct((k_blocks, rows // 2, 6 * HEAD_DIM), BF if k_blocks == q_blocks else F32),
        in_specs=[smem, smem, vmem, vmem, vmem, vmem] + [hbm] * len(others),
        out_specs=vmem,
        scratch_shapes=[
            pltpu.VMEM((q_rows, 128), BF),
            pltpu.VMEM((3, q_blocks, 128, rows), BF),
            pltpu.VMEM((k_rows, 128), BF),
            pltpu.VMEM((k_rows, 128), BF),
            pltpu.VMEM((q_rows, 128), BF),
            pltpu.VMEM((q_blocks, 128, rows), BF),
            pltpu.VMEM((3, 2 * rows, rows), F32),
            pltpu.VMEM((k_blocks // 2, 2, HEAD_DIM, rows), BF),
            pltpu.VMEM((HEAD_DIM, q_rows), F32),
            pltpu.VMEM((k_rows, HEAD_DIM), F32),
            pltpu.VMEM((k_rows, HEAD_DIM), F32),
        ],
        compiler_params=pltpu.CompilerParams(vmem_limit_bytes=VMEM_LIMIT),
        cost_estimate=pl.CostEstimate(
            flops=80 * q_rows * k_rows * HEAD_DIM, bytes_accessed=7_000_000, transcendentals=0
        ),
        name="attention_backward",
    )(info, slopes, qkv, attention, log_total, grads, *others)


def split_into(high_ref, low_ref, value):
    high = value.astype(BF)
    high_ref[...] = high
    if low_ref is not None:
        low_ref[...] = (value - high.astype(F32)).astype(BF)


PAIRS = ((0, 0), (1, 1), (2, 2), (0, 1), (0, 2), (1, 2))


def newton_schulz_steps(gram_ref, a0h, a0l, ah, al, bh, bl, qh, ql, q_s, a_s, p_s):
    size = gram_ref.shape[0]
    tile = 256
    count = size // tile
    row = lax.broadcasted_iota(jnp.int32, (size, size), 0)
    col = lax.broadcasted_iota(jnp.int32, (size, size), 1)
    eye = (row == col).astype(F32)
    trace = jnp.sum(jnp.sum(gram_ref[...] * eye, 0, keepdims=True), 1, keepdims=True)
    norm = jnp.sqrt(trace) + 1e-07
    a_s[...] = gram_ref[...] / (norm * norm)
    split_into(a0h, a0l, a_s[...])
    split_into(ah, al, a_s[...])

    def product(target, xh, xl, yh, yl, full, mirror, turned=False):
        for i in range(count):
            ri = slice(i * tile, (i + 1) * tile)
            for k in range(i if mirror else 0, count):
                rk = slice(k * tile, (k + 1) * tile)

                def term(x, y):
                    return dot(x[ri], y[rk], NT) if turned else dot(x[ri], y[:, rk])

                part = term(xh, yh)
                if full:
                    part = part + (term(xh, yl) + term(xl, yh))
                target[ri, rk] = part
                if mirror and k > i:
                    target[rk, ri] = part.T

    def advance(full, gram_full, first=False, last=False):
        product(p_s, ah, al, ah, al, full, True)
        poly = POLY_B * a_s[...] + POLY_C * p_s[...]
        if first:
            q_s[...] = poly + POLY_A * eye
        else:
            split_into(bh, bl if full else None, poly)
            product(p_s, bh, bl, qh, ql, full, False)
            q_s[...] = POLY_A * q_s[...] + p_s[...]
        if not last:
            split_into(qh, ql, q_s[...])
            product(p_s, a0h, a0l, qh, ql, gram_full, False, True)
            split_into(bh, bl, p_s[...])
            product(a_s, qh, ql, bh, bl, gram_full, True)
            split_into(ah, al, a_s[...])

    advance(False, False, first=True)

    @pl.loop(1, NS_STEPS - 2)
    def _(turn):
        advance(False, True)

    advance(True, True)
    advance(True, True, last=True)
    return norm


def ns_scratch(size):
    return [pltpu.VMEM((size, size), BF)] * 8 + [pltpu.VMEM((size, size), F32)] * 3


def newton_schulz_kernel(whole, which_ref, packed_ref, mine_ref, theirs_ref, *rest):
    out_ref, gram_s = rest[-13:-11]
    scratch = rest[-11:]
    tile = packed_ref.shape[3]
    half = tile // 2

    @pl.when(which_ref[0] == whole)
    def _():
        gram_s[...] = dot(mine_ref[...], mine_ref[...], NT) + dot(theirs_ref[...], theirs_ref[...], NT)

    @pl.when(which_ref[0] != whole)
    def _():
        for index, (i, k) in enumerate(PAIRS):
            block = jnp.concatenate([packed_ref[0, index], packed_ref[1, index]], 0)
            gram_s[i * tile : (i + 1) * tile, k * tile : (k + 1) * tile] = block
            if i != k:
                gram_s[k * tile : (k + 1) * tile, i * tile : (i + 1) * tile] = block.T

    norm = newton_schulz_steps(gram_s, *scratch)
    out_ref[...] = (scratch[8][...] / norm).astype(out_ref.dtype)


def newton_schulz(which, packed, mine, theirs, whole, *others):
    size = mine.shape[0]
    vmem = pl.BlockSpec(memory_space=pltpu.VMEM)
    smem = pl.BlockSpec(memory_space=pltpu.SMEM)
    return pl.pallas_call(
        functools.partial(newton_schulz_kernel, whole),
        out_shape=jax.ShapeDtypeStruct((size, size), BF),
        in_specs=[smem] + [vmem] * 3 + [pl.BlockSpec(memory_space=pl.ANY)] * len(others),
        out_specs=vmem,
        scratch_shapes=[pltpu.VMEM((size, size), F32)]
        + [pltpu.VMEM((size, size), BF)] * 8
        + [pltpu.VMEM((size, size), F32)] * 3,
        compiler_params=pltpu.CompilerParams(vmem_limit_bytes=VMEM_LIMIT),
        cost_estimate=pl.CostEstimate(flops=80 * size**3, bytes_accessed=7_000_000, transcendentals=0),
        name="newton_schulz",
    )(which, packed, mine, theirs, *others)


def gram_kernel(gated, out, which_ref, first_ref, second_ref, down_ref, packed_ref):
    tile = packed_ref.shape[3]
    half = tile // 2
    rest = gated - first_ref.shape[1]
    kinds = (
        lambda ri, rk: dot(first_ref[ri], first_ref[rk], NT) + dot(second_ref[ri, :rest], second_ref[rk, :rest], NT),
        lambda ri, rk: dot(down_ref[:, ri], down_ref[:, rk], TN),
        lambda ri, rk: dot(second_ref[ri, rest : rest + out], second_ref[rk, rest : rest + out], NT),
    )
    for index, gram in enumerate(kinds):

        @pl.when(jnp.minimum(which_ref[0], 2) == index)
        def _():
            for place, (i, k) in enumerate(PAIRS):
                block = gram(slice(i * tile, (i + 1) * tile), slice(k * tile, (k + 1) * tile))
                packed_ref[0, place] = block[:half]
                packed_ref[1, place] = block[half:]


def upper_gram(which, first, second, down, gated, out):
    vmem = pl.BlockSpec(memory_space=pltpu.VMEM)
    smem = pl.BlockSpec(memory_space=pltpu.SMEM)
    return pl.pallas_call(
        functools.partial(gram_kernel, gated, out),
        out_shape=jax.ShapeDtypeStruct((2, 6, 128, 256), F32),
        in_specs=[smem] + [vmem] * 3,
        out_specs=vmem,
        compiler_params=pltpu.CompilerParams(vmem_limit_bytes=VMEM_LIMIT),
        cost_estimate=pl.CostEstimate(flops=2 * first.shape[0] ** 2 * gated, bytes_accessed=6_000_000, transcendentals=0),
        name="upper_gram",
    )(which, first, second, down)


def update_kernel(scales, place_ref, *refs):
    halves, others = refs[:4], refs[4:8]
    first_ref, second_ref, down_ref, qkv_ref = refs[8:12]
    w_gated, w_down, w_out, w_qkv = refs[12:16]
    n_gated, n_down, n_out, n_qkv = refs[16:20]
    f_s, sems = refs[20:]
    which = place_ref[0]
    core = place_ref[1]
    half = halves[0].shape[0]
    copies = []
    for index, (mine, theirs) in enumerate(zip(halves, others)):
        m = jnp.bitwise_xor(which, index)
        for k, (ref, at) in enumerate(((mine, core), (theirs, 1 - core))):
            copy = pltpu.make_async_copy(
                ref, f_s.at[m, pl.ds(pl.multiple_of(at * half, half), half)], sems.at[2 * index + k]
            )
            copy.start()
            copies.append(copy)
    for copy in copies:
        copy.wait()
    third = first_ref.shape[1]
    gated = w_gated.shape[1] - third
    out = gated + w_out.shape[0]
    turned = (((0,), (1,)), ((), ()))

    def new(weight, scale, ortho):
        return weight * (1.0 - MUON_RATE * MUON_DECAY) - scale * ortho

    n_gated[:, :third] = new(w_gated[:, :third], scales[0], dot(f_s[0], first_ref[...]))
    n_gated[:, third:] = new(w_gated[:, third:], scales[0], dot(f_s[0], second_ref[:, :gated]))
    n_down[...] = new(w_down[...], scales[1], dot(down_ref[...], f_s[1], NT))
    n_out[...] = new(w_out[...], scales[2], dot(second_ref[:, gated:out], f_s[2], turned))
    n_qkv[...] = new(w_qkv[...], scales[3], dot(qkv_ref[...], f_s[3], turned))


def update(scales, place, halves, others, momenta, weights):
    size = halves[0].shape[1]
    vmem = pl.BlockSpec(memory_space=pltpu.VMEM)
    smem = pl.BlockSpec(memory_space=pltpu.SMEM)
    hbm = pl.BlockSpec(memory_space=pl.ANY)
    return pl.pallas_call(
        functools.partial(update_kernel, scales),
        out_shape=tuple(jax.ShapeDtypeStruct(weight.shape, F32) for weight in weights),
        in_specs=[smem] + [hbm] * 8 + [vmem] * 8,
        out_specs=(vmem,) * 4,
        scratch_shapes=[pltpu.VMEM((4, size, size), BF), pltpu.SemaphoreType.DMA((8,))],
        compiler_params=pltpu.CompilerParams(vmem_limit_bytes=VMEM_LIMIT),
        cost_estimate=pl.CostEstimate(flops=8 * size**3, bytes_accessed=28_000_000, transcendentals=0),
        name="update",
    )(place, *halves, *others, *momenta, *weights)


def project_kernel(
    groups, info_ref, vec_ref, x_ref, own_ref, far_ref, own_two, far_two, out_ref, group_ref, wo_ref, w_s, o_s
):
    core = info_ref[0]
    far = info_ref[1]
    unit = w_s.shape[2]
    seqs = out_ref.shape[0] // groups
    tokens = x_ref.shape[0] // seqs
    for a, refs in enumerate(((own_ref, far_ref), (own_two, far_two))):
        for z, ref in enumerate(refs):
            c = 2 * jnp.bitwise_xor(far, z) + jnp.bitwise_xor(core, a)
            for i in range(3):
                w_s[3 * c + i] = ref[:, i * unit : (i + 1) * unit]
            o_s[c] = ref[:, 3 * unit :]
    for g in range(groups):
        for role in range(3):
            group_ref[g, :, role * unit : (role + 1) * unit] = w_s[role * groups + g]
        part = dot(x_ref[...], group_ref[g])
        bias = jnp.concatenate(
            [jnp.zeros((1, 2 * unit), F32), vec_ref[0:1, g * unit : (g + 1) * unit]], 1
        )
        part = (part + bias).astype(BF)
        for b in range(seqs):
            fold(out_ref, b * groups + g, 0, part[b * tokens : (b + 1) * tokens])
    for c in range(4):
        wo_ref[:, c * unit : (c + 1) * unit] = o_s[c]


def project(info, vec, x, weights, groups, tokens):
    rows, width = x.shape
    unit = width // 4
    vmem = pl.BlockSpec(memory_space=pltpu.VMEM)
    smem = pl.BlockSpec(memory_space=pltpu.SMEM)
    return pl.pallas_call(
        functools.partial(project_kernel, groups),
        out_shape=(
            jax.ShapeDtypeStruct((groups * rows // tokens, tokens // 2, 6 * unit), BF),
            jax.ShapeDtypeStruct((groups, width, 3 * unit), BF),
            jax.ShapeDtypeStruct((width, width), BF),
        ),
        in_specs=[smem] + [vmem] * 6,
        out_specs=(vmem,) * 3,
        scratch_shapes=[pltpu.VMEM((12, width, unit), BF), pltpu.VMEM((4, width, unit), BF)],
        compiler_params=pltpu.CompilerParams(vmem_limit_bytes=VMEM_LIMIT),
        cost_estimate=pl.CostEstimate(
            flops=6 * rows * width * width, bytes_accessed=16_000_000, transcendentals=0
        ),
        name="project",
    )(info, vec, x, *weights)


def norm_back(grad, hat, scale, gain):
    inner = grad * gain
    mean = jnp.mean(inner, -1, keepdims=True)
    along = jnp.mean(inner * hat, -1, keepdims=True)
    return scale * (inner - mean - hat * along)


def feed_forward_kernel(
    groups,
    info_ref,
    vec_ref,
    x_ref,
    ctx_ref,
    cot_ref,
    wo_ref,
    own_ref,
    far_ref,
    own_two,
    far_two,
    out_ref,
    one_ref,
    gctx_ref,
    gvec_ref,
    keep_a,
    send_a,
    keep_b,
    send_b,
    w_s,
    ctx_s,
    hat_one,
    first_s,
    acc_s,
    gate_s,
    up_s,
    stage,
    wo_s,
    ffn_s,
    mixed_s,
    ggate_s,
    gup_s,
    sems,
):
    core = info_ref[0]
    far = info_ref[1]
    start = info_ref[2]
    rows, width = x_ref.shape
    unit = width // groups
    tokens = 2 * ctx_ref.shape[1]
    seqs = rows // tokens
    loads = []
    for a, refs in enumerate(((own_ref, far_ref), (own_two, far_two))):
        for z, ref in enumerate(refs):
            copy = pltpu.make_async_copy(ref.at[:, pl.ds(0, 3 * width)], w_s.at[a, z], sems.at[10 + 2 * a + z])
            copy.start()
            loads.append(copy)
    weights = (w_s.at[0], w_s.at[1])
    grads_a = (keep_a, send_a)
    grads_b = (keep_b, send_b)
    down_at = 2 * width
    part = rows

    def vec(i):
        return vec_ref[i : i + 1, :]

    for b in range(seqs):
        for g in range(groups):
            ctx_s[b * tokens : (b + 1) * tokens, g * unit : (g + 1) * unit] = unfold(ctx_ref, b * groups + g, 0, unit)
    residual = x_ref[...].astype(F32) + dot(ctx_s[...], wo_ref[...]) + vec(1)
    centre = residual - jnp.mean(residual, -1, keepdims=True)
    scale_one = lax.rsqrt(jnp.mean(centre * centre, -1, keepdims=True) + NORM_EPSILON)
    hat = centre * scale_one
    hat_one[...] = hat
    first = hat * vec(2) + vec(3)
    first_s[...] = first.astype(BF)
    acc_s[...] = first + vec(12)
    for copy in loads:
        copy.wait()

    def place(p_rel, s_rel):
        p = jnp.bitwise_xor(core, p_rel)
        s = jnp.bitwise_xor(core, s_rel)
        return p, 2 * p + s, pl.ds(pl.multiple_of(s * width, width), width)

    units = [(p, s) for p in range(2) for s in range(2)]
    half = math.sqrt(0.5)
    for index, (p_rel, s_rel) in enumerate(units):
        p, u, columns = place(p_rel, s_rel)
        down_z = jnp.bitwise_xor(p, far)

        @pl.loop(0, rows // part)
        def _(r):
            rs = pl.ds(pl.multiple_of(r * part, part), part)
            gate = dot(first_s[rs], weights[p_rel][far, :, columns]) + vec_ref[pl.ds(4 + u, 1), :]
            up = dot(first_s[rs], weights[p_rel][1 - far, :, columns]) + vec_ref[pl.ds(8 + u, 1), :]
            cdf = 0.5 + 0.5 * lax.erf(gate * half)
            pdf = jnp.exp(gate * gate * -0.5) * (1.0 / math.sqrt(2.0 * math.pi))
            gelu = gate * cdf
            gate_s[index, rs] = up * (cdf + gate * pdf)
            up_s[index, rs] = gelu
            mixed = (gelu * up).astype(BF)
            mixed_s[index, rs] = mixed
            acc_s[rs] += dot(mixed, weights[s_rel][down_z, :, down_at : down_at + width])

    residual = acc_s[...]
    centre = residual - jnp.mean(residual, -1, keepdims=True)
    scale_two = lax.rsqrt(jnp.mean(centre * centre, -1, keepdims=True) + NORM_EPSILON)
    hat = centre * scale_two
    row = lax.broadcasted_iota(jnp.int32, (rows, 1), 0)
    valid = jnp.zeros((rows, 1), F32)
    for b in range(seqs):
        inside = (row >= b * tokens) & (row < (b + 1) * tokens) & (start + row - b * tokens < info_ref[3 + b])
        valid = jnp.where(inside, 1.0, valid)
    out_ref[...] = ((hat * vec(13) + vec(14)) * valid).astype(BF)
    grad_second = cot_ref[...].astype(F32) * valid
    gvec_ref[13:14, :] = jnp.sum(grad_second * hat, 0, keepdims=True)
    gvec_ref[14:15, :] = jnp.sum(grad_second, 0, keepdims=True)
    gvec_ref[15:16, :] = jnp.zeros((1, width), F32)
    grad_two = norm_back(grad_second, hat, scale_two, vec(13))
    acc_s[...] = grad_two
    grad_ffn = grad_two.astype(BF)
    ffn_s[...] = grad_ffn
    gvec_ref[12:13, :] = jnp.sum(grad_ffn.astype(F32), 0, keepdims=True)

    copies = []

    def write(slot, value, target, z, columns):
        if len(copies) >= 6:
            copies[len(copies) - 6].wait()
        stage[slot] = value.astype(BF)
        copy = pltpu.make_async_copy(stage.at[slot], target.at[z, :, columns], sems.at[slot])
        copy.start()
        copies.append(copy)

    for index, (p_rel, s_rel) in enumerate(units):
        p, u, columns = place(p_rel, s_rel)
        down_z = jnp.bitwise_xor(p, far)
        grad_mixed = dot(ffn_s[...], weights[s_rel][down_z, :, down_at : down_at + width], NT)
        grad_gate = (grad_mixed * gate_s[index]).astype(BF)
        grad_up = (grad_mixed * up_s[index]).astype(BF)
        ggate_s[...] = grad_gate
        gup_s[...] = grad_up
        gvec_ref[pl.ds(4 + u, 1), :] = jnp.sum(grad_gate.astype(F32), 0, keepdims=True)
        gvec_ref[pl.ds(8 + u, 1), :] = jnp.sum(grad_up.astype(F32), 0, keepdims=True)
        acc_s[...] += dot(ggate_s[...], weights[p_rel][far, :, columns], NT)
        acc_s[...] += dot(gup_s[...], weights[p_rel][1 - far, :, columns], NT)
        slot = 3 * (index % 2)
        write(slot, dot(mixed_s[index], ffn_s[...], TN), grads_b[s_rel], down_z, pl.ds(0, width))
        write(slot + 1, dot(first_s[...], ggate_s[...], TN), grads_a[p_rel], far, columns)
        write(slot + 2, dot(first_s[...], gup_s[...], TN), grads_a[p_rel], 1 - far, columns)

    grad_first = acc_s[...]
    hat = hat_one[...]
    gvec_ref[2:3, :] = jnp.sum(grad_first * hat, 0, keepdims=True)
    gvec_ref[3:4, :] = jnp.sum(grad_first, 0, keepdims=True)
    grad_one = norm_back(grad_first, hat, scale_one, vec(2))
    one_ref[...] = grad_one
    grad_att = grad_one.astype(BF)
    gvec_ref[1:2, :] = jnp.sum(grad_att.astype(F32), 0, keepdims=True)
    grad_ctx = dot(grad_att, wo_ref[...], NT).astype(BF)
    gvec_ref[0:1, :] = jnp.sum(grad_ctx.astype(F32), 0, keepdims=True)
    for b in range(seqs):
        for g in range(groups):
            fold(gctx_ref, b * groups + g, 0, grad_ctx[b * tokens : (b + 1) * tokens, g * unit : (g + 1) * unit])
    grad_wo = dot(ctx_s[...], grad_att, TN).astype(BF)
    spare = wo_s.shape[2] - width // 4
    for c in range(4):
        part = grad_wo[:, c * (width // 4) : (c + 1) * (width // 4)]
        wo_s[c] = jnp.concatenate([part, jnp.zeros((width, spare), BF)], 1)
    last = []
    for a in range(2):
        for z in range(2):
            c = 2 * jnp.bitwise_xor(far, z) + jnp.bitwise_xor(core, a)
            copy = pltpu.make_async_copy(
                wo_s.at[c],
                grads_a[a].at[z, :, pl.ds(2 * width, wo_s.shape[2])],
                sems.at[6 + 2 * a + z],
            )
            copy.start()
            last.append(copy)
    for copy in copies[-6:] + last:
        copy.wait()


def feed_forward(info, vec, x, ctx, cot, wo, weights, groups):
    rows, width = x.shape
    vmem = pl.BlockSpec(memory_space=pltpu.VMEM)
    smem = pl.BlockSpec(memory_space=pltpu.SMEM)
    hbm = pl.BlockSpec(memory_space=pl.ANY)
    grads_a = jax.ShapeDtypeStruct((2, width, 2 * width + 256), BF)
    grads_b = jax.ShapeDtypeStruct((2, width, width), BF)
    return pl.pallas_call(
        functools.partial(feed_forward_kernel, groups),
        out_shape=(
            jax.ShapeDtypeStruct((rows, width), BF),
            jax.ShapeDtypeStruct((rows, width), F32),
            jax.ShapeDtypeStruct(ctx.shape, BF),
            jax.ShapeDtypeStruct((16, width), F32),
            grads_a,
            grads_a,
            grads_b,
            grads_b,
        ),
        in_specs=[smem] + [vmem] * 5 + [hbm] * 4,
        out_specs=(vmem,) * 4 + (hbm,) * 4,
        scratch_shapes=[
            pltpu.VMEM((2, 2, width, 3 * width), BF),
            pltpu.VMEM((rows, width), BF),
            pltpu.VMEM((rows, width), F32),
            pltpu.VMEM((rows, width), BF),
            pltpu.VMEM((rows, width), F32),
            pltpu.VMEM((4, rows, width), F32),
            pltpu.VMEM((4, rows, width), F32),
            pltpu.VMEM((6, width, width), BF),
            pltpu.VMEM((4, width, 256), BF),
            pltpu.VMEM((rows, width), BF),
            pltpu.VMEM((4, rows, width), BF),
            pltpu.VMEM((rows, width), BF),
            pltpu.VMEM((rows, width), BF),
            pltpu.SemaphoreType.DMA((14,)),
        ],
        compiler_params=pltpu.CompilerParams(vmem_limit_bytes=VMEM_LIMIT),
        cost_estimate=pl.CostEstimate(
            flops=60 * rows * width * width, bytes_accessed=34_000_000, transcendentals=0
        ),
        name="feed_forward",
    )(info, vec, x, ctx, cot, wo, *weights)


def qkv_grad_kernel(groups, heads, info_ref, x_ref, *refs):
    grad_refs = refs[:heads]
    rows_ref, keep_ref, send_ref, w_s = refs[-4:]
    core = info_ref[0]
    tokens = rows_ref.shape[1]
    seqs = rows_ref.shape[0] // groups
    unit = w_s.shape[2]
    for g in range(groups):
        total = None
        for b in range(seqs):
            owner = b * groups + g
            for role in range(3):
                for h in range(heads):
                    at = role * unit + h * HEAD_DIM
                    rows_ref[owner, :, at : at + HEAD_DIM] = unfold(grad_refs[h], owner, role * HEAD_DIM, HEAD_DIM)
            grads = rows_ref[owner]
            part = dot(x_ref[b * tokens : (b + 1) * tokens, :], grads, TN)
            total = part if total is None else total + part
        for role in range(3):
            w_s[role * groups + g] = total[:, role * unit : (role + 1) * unit].astype(BF)
    for a, ref in enumerate((keep_ref, send_ref)):
        for z in range(2):
            c = 2 * z + jnp.bitwise_xor(core, a)
            for i in range(3):
                at = (3 * z + i) * unit
                ref[:, at : at + unit] = w_s[3 * c + i]


def qkv_grad(info, x, grads, groups, *others):
    rows, width = x.shape
    heads = len(grads)
    unit = heads * HEAD_DIM
    vmem = pl.BlockSpec(memory_space=pltpu.VMEM)
    smem = pl.BlockSpec(memory_space=pltpu.SMEM)
    out = jax.ShapeDtypeStruct((width, 6 * unit), BF)
    return pl.pallas_call(
        functools.partial(qkv_grad_kernel, groups, heads),
        out_shape=(
            jax.ShapeDtypeStruct((grads[0].shape[0], 2 * grads[0].shape[1], 3 * unit), BF),
            out,
            out,
        ),
        in_specs=[smem] + [vmem] * (1 + heads) + [pl.BlockSpec(memory_space=pl.ANY)] * len(others),
        out_specs=(vmem,) * 3,
        scratch_shapes=[pltpu.VMEM((12, width, unit), BF)],
        compiler_params=pltpu.CompilerParams(vmem_limit_bytes=VMEM_LIMIT),
        cost_estimate=pl.CostEstimate(
            flops=6 * rows * width * width, bytes_accessed=9_000_000, transcendentals=0
        ),
        name="qkv_grad",
    )(info, x, *grads, *others)


def input_grad_kernel(groups, one_ref, grad_ref, group_ref, *rest):
    out_ref = rest[-1]
    tokens = grad_ref.shape[1]
    for b in range(grad_ref.shape[0] // groups):
        total = one_ref[b * tokens : (b + 1) * tokens, :]
        for g in range(groups):
            total = total + dot(grad_ref[b * groups + g], group_ref[g], NT)
        out_ref[b * tokens : (b + 1) * tokens, :] = total.astype(BF)


def input_grad(grad_one, grads, group, groups, *others):
    rows, width = grad_one.shape
    vmem = pl.BlockSpec(memory_space=pltpu.VMEM)
    return pl.pallas_call(
        functools.partial(input_grad_kernel, groups),
        out_shape=jax.ShapeDtypeStruct((rows, width), BF),
        in_specs=[vmem] * 3 + [pl.BlockSpec(memory_space=pl.ANY)] * len(others),
        out_specs=vmem,
        compiler_params=pltpu.CompilerParams(vmem_limit_bytes=VMEM_LIMIT),
        cost_estimate=pl.CostEstimate(
            flops=6 * rows * width * width, bytes_accessed=8_000_000, transcendentals=0
        ),
        name="input_grad",
    )(grad_one, grads, group, *others)


def on_device(
    hidden_in,
    cotangent,
    lengths,
    w_qkv,
    w_out,
    w_gated,
    w_down,
    vectors,
    mom_qkv,
    mom_out,
    mom_gated,
    mom_down,
    vec_first,
    vec_second,
):
    seqs, tokens, width = hidden_in.shape
    seq_count = lax.axis_size("seq")
    head_count = lax.axis_size("head")
    n = seq_count * head_count
    bits = n.bit_length() - 1
    length = tokens * n
    d = lax.axis_index("dp")
    seq_index = lax.axis_index("seq")
    head_index = lax.axis_index("head")
    j = seq_index * head_count + head_index
    core = lax.rem(d, 2)
    far = d // 2
    cols = w_qkv.shape[1]
    piece_rows = width // n

    def swap(value, over_dp=0, over_group=0):
        pairs = [
            (a * n + b, (a ^ over_dp) * n + (b ^ over_group)) for a in range(4) for b in range(n)
        ]
        return lax.ppermute(value, AXES, pairs)

    def bit_of(k):
        return lax.rem(j // (2**k), 2)

    def pick(value, index, axis=0):
        return lax.dynamic_index_in_dim(value, index, axis, keepdims=False)

    def join(cur, k, axis):
        other = swap(cur, 0, 2**k)
        first = bit_of(k) == 0
        return jnp.concatenate([jnp.where(first, cur, other), jnp.where(first, other, cur)], axis)

    def gather_group(piece, order):
        cur = piece.reshape((1,) * bits + piece.shape)
        for k in order:
            cur = join(cur, k, bits - 1 - k)
        return cur.reshape((n * piece.shape[0],) + piece.shape[1:])

    head_bits = head_count.bit_length() - 1

    def gather_rows(piece, axis):
        for k in range(head_bits):
            piece = join(piece, k, axis)
        return lax.all_gather(piece, "seq", axis=axis, tiled=True)

    def halve(value, k, axis):
        return pick(value, bit_of(k), axis), pick(value, 1 - bit_of(k), axis)

    def add(kept, got):
        return (kept.astype(F32) + got.astype(F32)).astype(BF)

    def rows_of(value):
        return lax.dynamic_slice_in_dim(value, j * piece_rows, piece_rows, 0)

    piece = swap(jnp.concatenate([rows_of(w_qkv), rows_of(w_out)], 1).astype(BF), 2)
    own_qo = jnp.concatenate([w_qkv, w_out], 1).astype(BF)
    rest_rows = width // seq_count

    def seq_rows(value):
        return lax.dynamic_slice_in_dim(value, seq_index * rest_rows, rest_rows, 0)

    rest = jnp.concatenate([seq_rows(w_gated), seq_rows(w_down)], 1).astype(BF)
    piece = after(piece, rest)
    rest = swap(rest, 2)
    own_rest = jnp.concatenate([w_gated.astype(BF), w_down.astype(BF)], 1)
    own_qo_two = swap(own_qo, 1)
    far_qo = gather_group(piece, range(bits))
    far_qo_two = swap(far_qo, 1)

    vec_low = vectors.astype(BF)
    vec_rel = [vec_low] + [swap(vec_low, k) for k in (1, 2, 3)]
    vec_pair = [
        jnp.where(core == 0, jnp.stack([vec_rel[a], vec_rel[a + 1]]), jnp.stack([vec_rel[a + 1], vec_rel[a]]))
        for a in (0, 2)
    ]
    vec = jnp.concatenate(
        [jnp.where(far == 0, vec_pair[0], vec_pair[1]), jnp.where(far == 0, vec_pair[1], vec_pair[0])]
    ).reshape(-1, width)
    vec = jnp.concatenate([vec.astype(F32), jnp.zeros((1, width), F32)])

    inner = math.gcd(n, seqs * HEADS)
    heads = seqs * HEADS // inner
    groups = inner // seqs
    unit = heads * HEAD_DIM
    me = lax.rem(j, inner)

    def exchange(blocks):
        if n == inner:
            return lax.all_to_all(blocks, ("seq", "head"), 0, 0, tiled=True)
        got = []
        for r in range(inner):
            block = pick(blocks, jnp.bitwise_xor(me, r))
            got.append(block if r == 0 else swap(block, 0, r))
        return jnp.take(jnp.stack(got), jnp.bitwise_xor(jnp.arange(inner), me), axis=0)

    info = jnp.concatenate([jnp.stack([core, far, j * tokens]), lengths]).astype(jnp.int32)
    x = hidden_in.reshape(seqs * tokens, width)
    owned, group_w, w_o = project(info, vec, x, (own_qo, far_qo, own_qo_two, far_qo_two), groups, tokens)
    own_rest_two = swap(own_rest, 1)
    qkv = exchange(owned)
    far_rest = lax.all_gather(after(rest, far_qo), "seq", axis=0, tiled=True)
    if n > inner:
        qkv = jnp.concatenate([qkv] + [swap(qkv, 0, s * inner) for s in range(1, n // inner)], 0)
    first_head = lax.rem(me, groups) * heads
    place = jnp.stack([j - me, pick(lengths, me // groups)]).astype(jnp.int32)
    head_ids = (first_head + jnp.arange(heads)).astype(F32)
    slopes = jnp.exp2(-8.0 * (head_ids + 1.0) / HEADS) * (64.0 / length)
    attention, attention_low, log_total = attention_forward(place, slopes, qkv, tokens, inner)
    context = exchange(attention_low)
    far_rest = after(far_rest, attention_low)
    far_rest_two = swap(far_rest, 1)
    hidden_out, grad_one, grad_context, grad_vec, keep_a, send_a, keep_b, send_b = feed_forward(
        info,
        vec,
        x,
        context,
        cotangent.reshape(seqs * tokens, width),
        w_o,
        (own_rest, far_rest, own_rest_two, far_rest_two),
        groups,
    )
    grad_owned = exchange(grad_context)

    third = keep_a.shape[2] // 2
    orders = [[(k + i) % bits for k in range(bits)] for i in (1, 2, 0)]
    bit_values = jnp.stack([bit_of(k) for k in range(bits)]).astype(jnp.int32)

    def by_bits(value):
        return value.reshape((2,) + (2,) * bits + (piece_rows, value.shape[2]))

    grad_vector = grad_vec[:15].reshape(2, 2, -1)
    vector = pick(grad_vector, core, 1), swap(pick(grad_vector, 1 - core, 1), 1)
    pairs = [(by_bits(keep_a), by_bits(swap(send_a, 1))), (by_bits(keep_b), by_bits(swap(send_b, 1)))]
    spans = [(0, 0, third), (0, third, 2 * third), (1, 0, keep_b.shape[2])]

    def split_step(step, pairs, spans, vector, *waits):
        if step < bits:
            places = [span + (bits - order[step], order[step]) for span, order in zip(spans, orders)]
        else:
            places = [span + (0, None) for span in spans]
        *values, vector = sum_split(places, bit_values, pairs, vector, waits)
        if step == bits:
            return values[::2], values[1::2], vector
        values = [
            value.reshape(value.shape[:place[3]] + (1,) + value.shape[place[3] :])
            for value, place in zip(values, [p for p in places for i in range(2)])
        ]
        got = [swap(value, 0, 2 ** order[step]) for value, order in zip(values[1::2], orders)]
        return list(zip(values[::2], got)), values[1::2], vector

    def backward(head, *others):
        return attention_backward(
            head, place, slopes, qkv, attention, log_total, grad_owned, tokens, inner, *others
        )

    def finish(grads):
        if n > inner:
            total = grads[:inner]
            for s in range(1, n // inner):
                total = total + swap(grads[s * inner : (s + 1) * inner], 0, s * inner)
            grads = total.astype(BF)
        return exchange(grads)

    def own_momentum():
        gated = rows_of(mom_gated)
        out = rows_of(mom_out)
        spare = jnp.zeros((piece_rows, 2 * third - gated.shape[1] - out.shape[1]), F32)
        return gated[:, :third], jnp.concatenate([gated[:, third:], out, spare], 1), rows_of(mom_down)

    old = own_momentum()
    head_rows = []
    waits = []
    for step in range(max(heads, bits)):
        if step < bits:
            pairs, sent, total = split_step(step, pairs, spans, vector, *waits)
            spans = [(i, 0, pair[0].shape[-1]) for i, pair in enumerate(pairs)]
            vector = total, swap(total, 0, 2**step)
            waits = [*sent, total]
        if step < heads:
            if step == heads - 1:
                waits.append(head_rows[0])
            back = backward(step, *waits)
            if step < heads - 1:
                head_rows.append(finish(back))
            waits = [back]
    own_parts, far_parts, total = split_step(bits, pairs, spans, vector, back)
    head_rows.append(finish(after(back, *far_parts)))
    parts = [
        (MUON_BETA * m + value.reshape(m.shape).astype(F32) + swap(other.reshape(m.shape), 2).astype(F32)).astype(BF)
        for m, value, other in zip(old, own_parts, far_parts)
    ]
    summed_vector = pick(total, far) + swap(pick(total, 1 - far), 2)

    def gather_parts(parts, step, *wait):
        others = [swap(part, 0, 2 ** order[step]) for part, order in zip(parts, orders)]
        places = [(bits - 1 - order[step], order[step]) for order in orders]
        return join_pairs(places, bit_values, parts, others, wait)

    shards = [part.reshape((1,) * bits + part.shape) for part in parts]

    grad_rows, keep, send = qkv_grad(info, x, head_rows, groups, *parts, summed_vector)
    shards = gather_parts(shards, 0, send)
    sum_qkv = add(keep, swap(send, 1))
    shards = gather_parts(shards, 1, sum_qkv)
    grad_in = input_grad(grad_one, grad_rows, group_w, groups, sum_qkv, *shards)
    sum_qkv = after(lax.psum_scatter(sum_qkv, "seq", scatter_dimension=0, tiled=True), grad_in)
    for step in range(2, bits):
        shards = gather_parts(shards, step, grad_in)
    shards = [part.reshape(width, part.shape[-1]) for part in shards]
    grad_in = grad_in.reshape(seqs, tokens, width)
    for k in reversed(range(head_bits)):
        kept, send = halve(sum_qkv.reshape(2, sum_qkv.shape[0] // 2, 2 * cols), k, 0)
        sum_qkv = add(kept, swap(send, 0, 2**k))
    old = MUON_BETA * rows_of(mom_qkv)
    near = far == 0
    old = jnp.concatenate([jnp.where(near, old, 0.0), jnp.where(near, 0.0, old)], 1)
    sum_qkv = (sum_qkv.astype(F32) + old).astype(BF)
    far_sum = swap(sum_qkv, 2)

    full_shapes = ((D, 3 * D), (D, D), (D, 2 * FF), (FF, D))
    factors = [MUON_RATE * 0.2 * math.sqrt(max(shape)) for shape in full_shapes]

    stride = seq_count // 4
    which = seq_index // stride
    kind = which.reshape(1).astype(jnp.int32)
    gated_at = w_gated.shape[1] - third
    out_at = gated_at + w_out.shape[1]
    packed = upper_gram(kind, *shards, w_gated.shape[1], w_out.shape[1])
    mine_m = gather_rows(add(sum_qkv, after(far_sum, packed)), 0)
    new_gated = jnp.concatenate([shards[0], shards[1][:, :gated_at]], 1).astype(F32)
    new_out = shards[1][:, gated_at:out_at].astype(F32)
    new_down = shards[2].astype(F32)
    count = len(PAIRS) // head_count
    part = lax.dynamic_slice_in_dim(packed, head_index * count, count, 1)
    part = pick(part, core) + swap(pick(part, 1 - core), 1)
    part = part + after(swap(part, 2), new_gated, new_down)
    theirs_m = swap(mine_m, 1)
    for k in range(head_bits):
        part = join(part, k, 0)
    other_core = swap(part, 1)
    packed = jnp.stack([jnp.where(core == 0, part, other_core), jnp.where(core == 0, other_core, part)])

    low_qkv = jnp.where(near, mine_m[:, :cols], mine_m[:, cols:])
    new_qkv = low_qkv.astype(F32)
    factor = newton_schulz(kind, packed, mine_m, theirs_m, 3, low_qkv)

    half_factor = pick(factor.reshape(2, width // 2, width), core)
    halves = [half_factor] + [swap(half_factor, 0, k * stride * head_count) for k in (1, 2, 3)]
    others = [swap(value, 1) for value in halves]
    new_w_gated, new_w_down, new_w_out, new_w_qkv = update(
        (factors[2], factors[3], factors[1], factors[0]),
        jnp.stack([which, core]).astype(jnp.int32),
        halves,
        others,
        (*shards, low_qkv),
        (w_gated, w_down, w_out.T, w_qkv.T),
    )
    moments = (new_qkv, new_out, new_gated, new_down)
    new_weights = (new_w_qkv.T, new_w_out.T, new_w_gated, new_w_down)
    first_new = ADAM_BETA_ONE * vec_first + (1.0 - ADAM_BETA_ONE) * summed_vector
    second_new = ADAM_BETA_TWO * vec_second + (1.0 - ADAM_BETA_TWO) * summed_vector * summed_vector
    first_hat = first_new / (1.0 - ADAM_BETA_ONE**STEP)
    second_hat = second_new / (1.0 - ADAM_BETA_TWO**STEP)
    vectors_new = vectors - ADAM_RATE * first_hat / (jnp.sqrt(second_hat) + ADAM_EPSILON)
    hidden_out = hidden_out.reshape(seqs, tokens, width)
    return (hidden_out, grad_in) + moments + new_weights + (first_new, second_new, vectors_new)


def solution(mesh):
    tokens = P("dp", ("seq", "head"), None)
    wide = P(None, "dp")
    tall = P("dp", None)
    flat = P("dp")
    in_specs = (tokens, tokens, flat) + (wide, wide, wide, tall, flat) + (wide, wide, wide, tall, flat, flat)
    out_specs = (tokens, tokens) + (wide, wide, wide, tall) * 2 + (flat, flat, flat)
    return jax.shard_map(on_device, mesh=mesh, in_specs=in_specs, out_specs=out_specs, check_vma=False)
```
